32 devices in a mesh: groups: 2 (over y), date: 4 (over z), tile: 2 (over x), head: 2 (over core).
Axes of the slice: x: 2, y: 2, z: 4, core: 2. Of those that a mesh axis runs over, the one named last changes fastest.
Arguments:
- tokens: bfloat16 [8, 8, 8, 64, 256], P('groups', 'tile', None, 'date'), parts along dimension 0, may hold values from -240 to 240
- cloud_mask: int32 [8, 8, 8, 64], P('groups', 'tile', None, 'date'), parts along dimension 0, may hold values from 0 to 1, as said below
- day_of_year: int32 [128], P(('groups', 'date')), parts along dimension 0, may hold values from 0 to 1460
- query: float32 [256], P('head'), may hold values from -6 to 6
- key_weight: bfloat16 [256, 256], P(None, 'head'), may hold values from -0.375 to 0.375
- value_weight: bfloat16 [256, 256], P(None, 'head'), may hold values from -0.375 to 0.375
- conv_first: bfloat16 [3, 3, 256, 256], P(None, None, None, 'head'), may hold values from -0.375 to 0.375
- conv_second: bfloat16 [3, 3, 256, 256], P(None, None, None, 'head'), may hold values from -0.1875 to 0.1875
Outputs:
- feature_map: bfloat16 [8, 8, 8, 256], P(('groups', 'date'), 'tile', None, 'head'), parts along dimension 0
The draws below stay inside these ranges and needn't reach their ends.
There are 2 independent parts, one for each index of `groups`. The reference program is written for one: setup_inputs(seed, part) draws one part's arguments, and reference() takes and returns one part's arrays. A program takes and returns all parts, laid end to end along the dimension named above; an argument that names none is the same for every part. Nothing has to cross between parts.
Inputs may be any that keep to these rules, and one draw needn't show every extreme that they name: `cloud_mask`: a pixel may be clouded on all 64 dates.
All inputs are finite; a program needn't handle non-finite values.
Results may differ from the reference program's by a relative error of at most 0.012.
The reference program's roundings to bfloat16 on the way (of `inputs`, `pooled` and `hidden`) count: a program that leaves them out, or rounds other values in their place, can miss the bound.
Values may be sent and summed in bfloat16 or wider, within the bound.
No kernel may reach another device: no remote copies, remote signals or barrier semaphores. Data moves between devices by JAX's collectives and lax.ppermute only.
A program may use at most 128 MiB of HBM per device.

```python
import jax
import jax.numpy as jnp
from jax import lax

D = 256
HEADS = 8
HSIZE = 32
DATES = 64
TILES = 4
H = 8
WIDTH = 8


def draw_tokens(key, part):
    shape = (TILES, H, WIDTH, DATES, D)
    first = jax.random.fold_in(jax.random.fold_in(key, 17), 0)
    return jnp.clip(jax.random.normal(first, shape, jnp.float32), -6.0, 6.0).astype(jnp.bfloat16)


def draw_cloud_mask(key, part):
    first, second = jax.random.split(jax.random.fold_in(key, 29), 2)
    clear = jax.random.randint(first, (TILES, H, WIDTH, DATES), 0, 4) != 0
    covered = jax.random.randint(second, (TILES, H, WIDTH), 0, 16) == 0
    return (clear & jnp.logical_not(covered)[..., None]).astype(jnp.int32)


def plant(result, stream_key, least, top_value):
    longest = result.shape.index(max(result.shape))
    spots = []
    for shift in (0, 1):
        where = [jax.random.randint(jax.random.fold_in(stream_key, axis), (), 0, length) for axis, length in enumerate(result.shape)]
        where[longest] = (where[longest] + shift) % result.shape[longest]
        spots.append(tuple(where))
    return result.at[spots[0]].set(least).at[spots[1]].set(top_value)


def steps_of(rng, extent, cuts, smallest, high):
    gain = 1.0
    for dim, shards_of in cuts:
        draws = jax.random.uniform(jax.random.fold_in(jax.random.fold_in(rng, 6), dim), (shards_of,), jnp.float32, smallest / len(cuts), high / len(cuts))
        gain = gain * jnp.repeat(jnp.exp(draws), extent[dim] // shards_of).reshape((-1,) + (1,) * (len(extent) - 1 - dim))
    return gain


def bell_draw(own_key, extent, spread, most, cuts=(), kind=jnp.bfloat16):
    drawn = jax.random.normal(own_key, extent, jnp.float32) * spread
    if len(cuts) > 0:
        drawn = steps_of(own_key, extent, cuts, -0.22, 0.18) * drawn
    return jnp.clip(drawn, min=-most, max=most).astype(kind)


def setup_inputs(seed: int = 0, part: int = 0) -> dict:
    splits = jax.random.split(jax.random.key(seed), 9)
    part_keys = jax.random.split(jax.random.fold_in(splits[8], part), 9)
    tokens = draw_tokens(jax.random.fold_in(jax.random.fold_in(splits[8], part), 71), part)
    cloud_mask = draw_cloud_mask(jax.random.fold_in(jax.random.fold_in(splits[8], part), 71), part)
    day_of_year = plant(jax.random.randint(part_keys[2], (DATES,), 0, 1461), jax.random.fold_in(part_keys[2], 1), 0, 1460).astype(jnp.int32)
    query = bell_draw(splits[3], (D,), 1.5, 6.0, ((0, 2),), jnp.float32)
    key_weight = bell_draw(splits[4], (D, D), D ** -0.5, 0.375, ((1, 2),))
    value_weight = bell_draw(splits[5], (D, D), D ** -0.5, 0.375, ((1, 2),))
    conv_first = bell_draw(splits[6], (3, 3, D, D), D ** -0.5, 0.375, ((3, 2),))
    conv_second = bell_draw(splits[7], (3, 3, D, D), (4 * D) ** -0.5, 0.1875, ((3, 2),))
    return dict(tokens=tokens, cloud_mask=cloud_mask, day_of_year=day_of_year, query=query, key_weight=key_weight, value_weight=value_weight, conv_first=conv_first, conv_second=conv_second)


cloud_penalty = 6.0

def encoding(day_of_year, width):
    chan = jnp.arange(width)
    expo = (2 * (chan // 2)).astype(jnp.float32) / width
    freq = jnp.power(jnp.float32(1000.0), -expo)
    angle = day_of_year.astype(jnp.float32)[:, None] * freq[None, :]
    return jnp.where((chan % 2 == 0)[None, :], jnp.sin(angle), jnp.cos(angle))

def convolve(field, kernel):
    rows, cols = (field.shape[1], field.shape[2])
    padded = jnp.pad(field, ((0, 0), (1, 1), (1, 1), (0, 0)))
    total = jnp.zeros((field.shape[0] * rows * cols, kernel.shape[3]), jnp.float32)
    for arow in range(3):
        for bcol in range(3):
            piece = padded[:, arow:arow + rows, bcol:bcol + cols, :].reshape(-1, field.shape[3])
            total = total + jnp.dot(piece, kernel[arow, bcol], preferred_element_type=jnp.float32)
    return total.reshape(field.shape[0], rows, cols, kernel.shape[3])

def reference(tokens, cloud_mask, day_of_year, query, key_weight, value_weight, conv_first, conv_second):
    table = encoding(day_of_year, D)
    query_heads = query.astype(jnp.float32).reshape(HEADS, HSIZE)

    def one_tile(pair):
        feats, clear = pair
        inputs = (feats.astype(jnp.float32) + table[None, None]).astype(jnp.bfloat16).reshape(-1, D)
        keys = jnp.dot(inputs, key_weight, preferred_element_type=jnp.float32).reshape(H * WIDTH, DATES, HEADS, HSIZE)
        vals = jnp.dot(inputs, value_weight, preferred_element_type=jnp.float32).reshape(H * WIDTH, DATES, HEADS, HSIZE)
        score = lax.optimization_barrier(jnp.sum(keys * query_heads[None, None], axis=-1)) / jnp.sqrt(jnp.float32(HSIZE))
        score = score - cloud_penalty * (1.0 - clear.reshape(H * WIDTH, DATES, 1).astype(jnp.float32))
        attn = jax.nn.softmax(score, axis=1)
        pooled = lax.optimization_barrier(jnp.sum(attn[..., None] * vals, axis=1))
        return pooled.reshape(H, WIDTH, D).astype(jnp.bfloat16)
    pooled = lax.map(one_tile, (tokens, cloud_mask))
    hidden = jax.nn.relu(convolve(pooled, conv_first)).astype(jnp.bfloat16)
    return convolve(hidden, conv_second).astype(jnp.bfloat16)
```

```python
import functools

import jax
import jax.numpy as jnp
from jax import lax
from jax.experimental import pallas as pl
from jax.experimental.pallas import tpu as pltpu
from jax.sharding import PartitionSpec as P

HSIZE = 32
LANES = 128
PENALTY = 6.0
F32 = jnp.float32
BF16 = jnp.bfloat16


def encoding(day_of_year, width):
    chan = jnp.arange(width)
    expo = (2 * (chan // 2)).astype(F32) / width
    freq = jnp.power(F32(1000.0), -expo)
    angle = day_of_year.astype(F32)[:, None] * freq[None, :]
    return jnp.where((chan % 2 == 0)[None, :], jnp.sin(angle), jnp.cos(angle))


def iota(shape, dim):
    return lax.broadcasted_iota(jnp.int32, shape, dim)


def split3(value):
    high = value.astype(BF16)
    rest = value - high.astype(F32)
    mid = rest.astype(BF16)
    low = (rest - mid.astype(F32)).astype(BF16)
    return high, mid, low


def same_head(rows):
    row = lax.rem(iota((rows, LANES), 0), LANES)
    return (row // HSIZE == iota((rows, LANES), 1) // HSIZE).astype(BF16)


def dot(a, b):
    return jnp.dot(a, b, preferred_element_type=F32)


def attend_kernel(
    pixels, dates, copies, tokens, mask, table, query, keyw, valw, out, weights, score, vals
):
    @pl.when(pl.program_id(0) == 0)
    def _():
        scaled = keyw[...].astype(F32) * (query[...] * F32(HSIZE**-0.5))
        spread = same_head(LANES)
        high, mid, low = split3(scaled)
        folded = dot(high, spread) + (dot(mid, spread) + dot(low, spread))
        high, mid, low = split3(folded)
        weights[:, 0:LANES] = high
        weights[:, LANES : 2 * LANES] = mid
        weights[:, 2 * LANES : 3 * LANES] = low
        weights[:, 3 * LANES : 4 * LANES] = valw[...]

    width = tokens.shape[-1]
    feats = tokens[...].reshape(pixels, dates, width).astype(F32) + table[...][None]
    inputs = feats.astype(BF16).reshape(pixels * dates, width)
    both = dot(inputs, weights[...])
    score[...] = both[:, 0:LANES] + (both[:, LANES : 2 * LANES] + both[:, 2 * LANES : 3 * LANES])
    vals[...] = both[:, 3 * LANES : 4 * LANES]
    clear = mask[...].reshape(pixels, dates).astype(F32)
    cloud = PENALTY * (1.0 - clear)
    rows = [
        score[pl.ds(t, pixels, stride=dates), :] - cloud[:, t : t + 1] for t in range(dates)
    ]
    top = functools.reduce(jnp.maximum, rows)
    total = jnp.zeros((pixels, LANES), F32)
    summed = jnp.zeros((pixels, LANES), F32)
    for t in range(dates):
        expo = jnp.exp(rows[t] - top)
        total = total + expo
        summed = summed + expo * vals[pl.ds(t, pixels, stride=dates), :]
    part = (summed / total).astype(BF16)
    level = top + jnp.log(total)
    own = lax.rem(iota((pixels, LANES), 1), HSIZE) == iota((pixels, LANES), 0)
    packed = jnp.sum(jnp.where(own, level, 0.0), axis=0, keepdims=True)
    high, mid, low = split3(packed)
    row = iota((16, LANES), 0)
    tail = jnp.where(
        row == 0,
        high.astype(F32),
        jnp.where(row == 1, mid.astype(F32), jnp.where(row == 2, low.astype(F32), 0.0)),
    ).astype(BF16)
    for copy in range(copies):
        out[0, copy, 0:pixels, :] = part
        out[0, copy, pixels : pixels + 16, :] = tail


def attend(tokens, cloud_mask, table, query, key_weight, value_weight, copies):
    tiles, rows, cols, dates, width = tokens.shape
    pixels = rows * cols
    tokens = tokens.reshape(tiles, pixels * dates, width)
    mask = cloud_mask.reshape(tiles, pixels, dates)
    whole = lambda *shape: pl.BlockSpec(shape, lambda i: (0,) * len(shape))
    return pl.pallas_call(
        functools.partial(attend_kernel, pixels, dates, copies),
        grid=(tiles,),
        in_specs=[
            pl.BlockSpec((1, pixels * dates, width), lambda i: (i, 0, 0)),
            pl.BlockSpec((1, pixels, dates), lambda i: (i, 0, 0)),
            whole(dates, width),
            whole(1, LANES),
            whole(width, LANES),
            whole(width, LANES),
        ],
        out_specs=pl.BlockSpec((1, copies, pixels + 16, LANES), lambda i: (i, 0, 0, 0)),
        out_shape=jax.ShapeDtypeStruct((tiles, copies, pixels + 16, LANES), BF16),
        scratch_shapes=[
            pltpu.VMEM((width, 4 * LANES), BF16),
            pltpu.VMEM((pixels * dates, LANES), F32),
            pltpu.VMEM((pixels * dates, LANES), F32),
        ],
        compiler_params=pltpu.CompilerParams(vmem_limit_bytes=16 * 2**20),
    )(tokens, mask, table, query.reshape(1, LANES), key_weight, value_weight)


def merge(blocks, pixels, first, count):
    levels = [jnp.sum(block[pixels : pixels + 16, :].astype(F32), axis=0, keepdims=True) for block in blocks]
    best = functools.reduce(jnp.maximum, levels)
    shares = [jnp.exp(level - best) for level in levels]
    total = functools.reduce(jnp.add, shares)
    own = lax.rem(iota((count, LANES), 1), HSIZE) == iota((count, LANES), 0) + first
    spread = same_head(2 * LANES)
    pooled = jnp.zeros((count, LANES), F32)
    for block, share in zip(blocks, shares):
        share = share / total
        high = share.astype(BF16).astype(F32)
        both = jnp.concatenate([jnp.where(own, high, 0.0), jnp.where(own, share - high, 0.0)], axis=1)
        pooled = pooled + dot(both.astype(BF16), spread) * block[first : first + count, :].astype(F32)
    return pooled.astype(BF16).astype(F32)


def columns(field, cols):
    count = field.shape[0]
    col = lax.rem(iota(field.shape, 0), cols)
    left = jnp.where(col == 0, 0.0, pltpu.roll(field, 1, 0))
    right = jnp.where(col == cols - 1, 0.0, pltpu.roll(field, count - 1, 0))
    return jnp.concatenate([left, field, right], axis=1).astype(BF16)


def stencil(field, kernel, cols):
    count = field.shape[0] - 2 * cols
    return sum(dot(field, kernel[a])[a * cols : a * cols + count] for a in range(3))


def convolve_kernel(pixels, cols, place, got, first, other, second, out):
    dates, slabs, heads = got.shape[:3]
    slab, head = place[0], place[1]
    above, below = jnp.maximum(slab - 1, 0), jnp.minimum(slab + 1, slabs - 1)
    halo = 2 * cols

    def region(source, start, count):
        return jnp.concatenate(
            [merge([got[d, source, h] for d in range(dates)], pixels, start, count) for h in range(heads)],
            axis=1,
        )

    field = jnp.concatenate(
        [
            jnp.where(slab > 0, region(above, pixels - halo, halo), 0.0),
            region(slab, 0, pixels),
            jnp.where(slab < slabs - 1, region(below, 0, halo), 0.0),
        ],
        axis=0,
    )
    wide = columns(field, cols)
    mine = stencil(wide, first, cols)
    theirs = stencil(wide, other, cols)
    hidden = jnp.concatenate(
        [jnp.where(head == 0, mine, theirs), jnp.where(head == 0, theirs, mine)], axis=1
    )
    count = pixels + 2 * cols
    row = iota(hidden.shape, 0)
    inside = jnp.logical_and(
        jnp.logical_or(row >= cols, slab > 0), jnp.logical_or(row < count - cols, slab < slabs - 1)
    )
    hidden = jnp.where(inside, jnp.maximum(hidden, 0.0), 0.0).astype(BF16).astype(F32)
    out[...] = stencil(columns(hidden, cols), second, cols).astype(BF16)


def convolve(got, place, first, other, second, pixels, cols):
    return pl.pallas_call(
        functools.partial(convolve_kernel, pixels, cols),
        in_specs=[pl.BlockSpec(memory_space=pltpu.SMEM)] + [pl.BlockSpec(memory_space=pltpu.VMEM)] * 4,
        out_specs=pl.BlockSpec(memory_space=pltpu.VMEM),
        out_shape=jax.ShapeDtypeStruct((pixels, second.shape[-1]), BF16),
        compiler_params=pltpu.CompilerParams(vmem_limit_bytes=32 * 2**20),
    )(place, got, first, other, second)


def local(slabs, heads, tokens, cloud_mask, day_of_year, query, key_weight, value_weight, conv_first, conv_second):
    tiles, rows, cols, dates, width = tokens.shape
    pixels = rows * cols
    first = conv_first.reshape(3, 3 * width, -1)
    second = conv_second.reshape(3, 3 * width, -1)
    other = lax.ppermute(first, "head", [(i, heads - 1 - i) for i in range(heads)])
    table = encoding(day_of_year, width)
    sent = attend(tokens, cloud_mask, table, query, key_weight, value_weight, slabs * heads)
    got = lax.all_to_all(
        sent.reshape(tiles * slabs * heads, pixels + 16, LANES),
        ("date", "tile", "head"),
        split_axis=0,
        concat_axis=0,
        tiled=True,
    ).reshape(tiles, slabs, heads, pixels + 16, LANES)
    place = jnp.stack([lax.axis_index("tile"), lax.axis_index("head")]).astype(jnp.int32)
    out = convolve(got, place, first, other, second, pixels, cols)
    return out.reshape(1, rows, cols, -1)


def solution(mesh):
    in_specs = (
        P("groups", "tile", None, "date", None),
        P("groups", "tile", None, "date"),
        P(("groups", "date")),
        P("head"),
        P(None, "head"),
        P(None, "head"),
        P(None, None, None, "head"),
        P(None, None, None, "head"),
    )
    out_specs = P(("groups", "date"), "tile", None, "head")
    body = functools.partial(local, mesh.shape["tile"], mesh.shape["head"])
    return jax.shard_map(body, mesh=mesh, in_specs=in_specs, out_specs=out_specs, check_vma=False)
```

```python
import functools
import math

import jax
import jax.numpy as jnp
from jax import lax
from jax.experimental import pallas as pl
from jax.experimental.pallas import tpu as pltpu
from jax.sharding import PartitionSpec as P

HSIZE = 32
LANES = 128
PENALTY = 6.0
F32 = jnp.float32
BF16 = jnp.bfloat16


def iota(shape, dim):
    return lax.broadcasted_iota(jnp.int32, shape, dim)


def split3(value):
    high = value.astype(BF16)
    rest = value - high.astype(F32)
    mid = rest.astype(BF16)
    low = (rest - mid.astype(F32)).astype(BF16)
    return high, mid, low


def same_head(rows):
    row = lax.rem(iota((rows, LANES), 0), LANES)
    return (row // HSIZE == iota((rows, LANES), 1) // HSIZE).astype(BF16)


def dot(a, b):
    return jnp.dot(a, b, preferred_element_type=F32)


def encoding_rows(days, dates, width):
    row, chan = iota((dates, width), 0), iota((dates, width), 1)
    even = lax.rem(chan, 2) == 0
    expo = (chan - lax.rem(chan, 2)).astype(F32) * F32(math.log(1000.0) / width)
    day = jnp.zeros((dates, width), F32)
    for t in range(dates):
        day = jnp.where(row == t, days[t].astype(F32), day)
    angle = day * jnp.exp(-expo)
    return jnp.where(even, jnp.sin(angle), jnp.cos(angle))


def attend_kernel(
    pixels, dates, copies, tokens_hbm, mask_hbm, days_hbm, query_hbm, keyw_hbm, valw_hbm, out,
    tokens, mask, days, query, keyw, weights, score, vals, sems, token_sems,
):
    tiles, width = tokens.shape[0], tokens.shape[-1]
    columns = pl.ds(3 * LANES, LANES)
    small = [
        pltpu.make_async_copy(days_hbm, days, sems.at[0]),
        pltpu.make_async_copy(query_hbm, query, sems.at[1]),
        pltpu.make_async_copy(keyw_hbm, keyw, sems.at[2]),
        pltpu.make_async_copy(valw_hbm, weights.at[:, columns], sems.at[3]),
        pltpu.make_async_copy(mask_hbm, mask, sems.at[4]),
    ]
    for copy in small:
        copy.start()
    loads = lambda i: pltpu.make_async_copy(tokens_hbm.at[i], tokens.at[i], token_sems.at[i])
    for i in range(tiles):
        loads(i).start()
    small[0].wait()
    table = encoding_rows(days, dates, width)
    small[1].wait()
    small[2].wait()
    scaled = keyw[...].astype(F32) * (query[...] * F32(HSIZE**-0.5))
    spread = same_head(LANES)
    high, mid, low = split3(scaled)
    folded = dot(high, spread) + (dot(mid, spread) + dot(low, spread))
    high, mid, low = split3(folded)
    weights[:, 0:LANES] = high
    weights[:, LANES : 2 * LANES] = mid
    weights[:, 2 * LANES : 3 * LANES] = low
    small[3].wait()
    small[4].wait()

    def one(i):
        loads(i).wait()
        feats = tokens[i].reshape(pixels, dates, width).astype(F32) + table[None]
        inputs = feats.astype(BF16).reshape(pixels * dates, width)
        both = dot(inputs, weights[...])
        score[...] = both[:, 0:LANES] + (both[:, LANES : 2 * LANES] + both[:, 2 * LANES : 3 * LANES])
        vals[...] = both[:, 3 * LANES : 4 * LANES]
        cloud = PENALTY * (1.0 - mask[i].astype(F32))
        rows = [
            score[pl.ds(t, pixels, stride=dates), :] - cloud[:, t : t + 1] for t in range(dates)
        ]
        top = functools.reduce(jnp.maximum, rows)
        total = jnp.zeros((pixels, LANES), F32)
        summed = jnp.zeros((pixels, LANES), F32)
        for t in range(dates):
            expo = jnp.exp(rows[t] - top)
            total = total + expo
            summed = summed + expo * vals[pl.ds(t, pixels, stride=dates), :]
        part = (summed / total).astype(BF16)
        level = top + jnp.log(total)
        own = lax.rem(iota((pixels, LANES), 1), HSIZE) == iota((pixels, LANES), 0)
        packed = jnp.sum(jnp.where(own, level, 0.0), axis=0, keepdims=True)
        high, mid, low = split3(packed)
        row = iota((16, LANES), 0)
        tail = jnp.where(
            row == 0,
            high.astype(F32),
            jnp.where(row == 1, mid.astype(F32), jnp.where(row == 2, low.astype(F32), 0.0)),
        ).astype(BF16)
        for copy in range(copies):
            out[i, copy, 0:pixels, :] = part
            out[i, copy, pixels : pixels + 16, :] = tail

    if tiles <= 4:
        for i in range(tiles):
            one(i)
    else:
        pl.loop(0, tiles)(one)


def attend(tokens, cloud_mask, day_of_year, query, key_weight, value_weight, copies):
    tiles, rows, cols, dates, width = tokens.shape
    pixels = rows * cols
    tokens = tokens.reshape(tiles, pixels * dates, width)
    mask = cloud_mask.reshape(tiles, pixels, dates)
    return pl.pallas_call(
        functools.partial(attend_kernel, pixels, dates, copies),
        in_specs=[pl.BlockSpec(memory_space=pltpu.HBM)] * 6,
        out_specs=pl.BlockSpec(memory_space=pltpu.VMEM),
        out_shape=jax.ShapeDtypeStruct((tiles, copies, pixels + 16, LANES), BF16),
        scratch_shapes=[
            pltpu.VMEM(tokens.shape, BF16),
            pltpu.VMEM(mask.shape, jnp.int32),
            pltpu.SMEM(day_of_year.shape, jnp.int32),
            pltpu.VMEM((1, LANES), F32),
            pltpu.VMEM((width, LANES), BF16),
            pltpu.VMEM((width, 4 * LANES), BF16),
            pltpu.VMEM((pixels * dates, LANES), F32),
            pltpu.VMEM((pixels * dates, LANES), F32),
            pltpu.SemaphoreType.DMA((5,)),
            pltpu.SemaphoreType.DMA((tiles,)),
        ],
        compiler_params=pltpu.CompilerParams(vmem_limit_bytes=60 * 2**20),
    )(tokens, mask, day_of_year, query.reshape(1, LANES), key_weight, value_weight)


def merge(blocks, pixels, first, count):
    levels = [jnp.sum(block[pixels : pixels + 16, :].astype(F32), axis=0, keepdims=True) for block in blocks]
    best = functools.reduce(jnp.maximum, levels)
    shares = [jnp.exp(level - best) for level in levels]
    total = functools.reduce(jnp.add, shares)
    own = lax.rem(iota((count, LANES), 1), HSIZE) == iota((count, LANES), 0) + first
    spread = same_head(2 * LANES)
    pooled = jnp.zeros((count, LANES), F32)
    for block, share in zip(blocks, shares):
        share = share / total
        high = share.astype(BF16).astype(F32)
        both = jnp.concatenate([jnp.where(own, high, 0.0), jnp.where(own, share - high, 0.0)], axis=1)
        pooled = pooled + dot(both.astype(BF16), spread) * block[first : first + count, :].astype(F32)
    return pooled.astype(BF16).astype(F32)


def columns(field, cols):
    count = field.shape[0]
    col = lax.rem(iota(field.shape, 0), cols)
    left = jnp.where(col == 0, 0.0, pltpu.roll(field, 1, 0))
    right = jnp.where(col == cols - 1, 0.0, pltpu.roll(field, count - 1, 0))
    return jnp.concatenate([left, field, right], axis=1).astype(BF16)


def stencil(field, kernel, cols):
    count = field.shape[0] - 2 * cols
    return sum(dot(field, kernel[a])[a * cols : a * cols + count] for a in range(3))


def convolve_kernel(pixels, cols, place, got, swapped, first, other, second, out):
    dates, slabs = got.shape[:2]
    slab, head = place[0], place[1]
    above, below = jnp.maximum(slab - 1, 0), jnp.minimum(slab + 1, slabs - 1)
    halo = 2 * cols

    def in_order(mine, theirs):
        return jnp.concatenate(
            [jnp.where(head == 0, mine, theirs), jnp.where(head == 0, theirs, mine)], axis=1
        )

    def region(source, start, count):
        mine, theirs = (
            merge([half[d, source] for d in range(dates)], pixels, start, count) for half in (got, swapped)
        )
        return in_order(mine, theirs)

    field = jnp.concatenate(
        [
            jnp.where(slab > 0, region(above, pixels - halo, halo), 0.0),
            region(slab, 0, pixels),
            jnp.where(slab < slabs - 1, region(below, 0, halo), 0.0),
        ],
        axis=0,
    )
    wide = columns(field, cols)
    mine = stencil(wide, first, cols)
    theirs = stencil(wide, other, cols)
    hidden = in_order(mine, theirs)
    count = pixels + 2 * cols
    row = iota(hidden.shape, 0)
    inside = jnp.logical_and(
        jnp.logical_or(row >= cols, slab > 0), jnp.logical_or(row < count - cols, slab < slabs - 1)
    )
    hidden = jnp.where(inside, jnp.maximum(hidden, 0.0), 0.0).astype(BF16).astype(F32)
    out[...] = stencil(columns(hidden, cols), second, cols).astype(BF16)


def convolve(got, swapped, place, first, other, second, pixels, cols):
    return pl.pallas_call(
        functools.partial(convolve_kernel, pixels, cols),
        in_specs=[pl.BlockSpec(memory_space=pltpu.SMEM)] + [pl.BlockSpec(memory_space=pltpu.VMEM)] * 5,
        out_specs=pl.BlockSpec(memory_space=pltpu.VMEM),
        out_shape=jax.ShapeDtypeStruct((pixels, second.shape[-1]), BF16),
        compiler_params=pltpu.CompilerParams(vmem_limit_bytes=32 * 2**20),
    )(place, got, swapped, first, other, second)


def local(slabs, heads, tokens, cloud_mask, day_of_year, query, key_weight, value_weight, conv_first, conv_second):
    tiles, rows, cols, dates, width = tokens.shape
    pixels = rows * cols
    first = conv_first.reshape(3, 3 * width, -1)
    second = conv_second.reshape(3, 3 * width, -1)
    swap = [(i, heads - 1 - i) for i in range(heads)]
    other = lax.ppermute(first, "head", swap)
    sent = attend(tokens, cloud_mask, day_of_year, query, key_weight, value_weight, slabs)
    got = lax.all_to_all(
        sent.reshape(tiles * slabs, pixels + 16, LANES),
        ("date", "tile"),
        split_axis=0,
        concat_axis=0,
        tiled=True,
    ).reshape(tiles, slabs, pixels + 16, LANES)
    swapped = lax.ppermute(got, "head", swap)
    place = jnp.stack([lax.axis_index("tile"), lax.axis_index("head")]).astype(jnp.int32)
    out = convolve(got, swapped, place, first, other, second, pixels, cols)
    return out.reshape(1, rows, cols, -1)


def solution(mesh):
    in_specs = (
        P("groups", "tile", None, "date", None),
        P("groups", "tile", None, "date"),
        P(("groups", "date")),
        P("head"),
        P(None, "head"),
        P(None, "head"),
        P(None, None, None, "head"),
        P(None, None, None, "head"),
    )
    out_specs = P(("groups", "date"), "tile", None, "head")
    body = functools.partial(local, mesh.shape["tile"], mesh.shape["head"])
    return jax.shard_map(body, mesh=mesh, in_specs=in_specs, out_specs=out_specs, check_vma=False)
```

```python
import functools
import math

import jax
import jax.numpy as jnp
from jax import lax
from jax.experimental import pallas as pl
from jax.experimental.pallas import tpu as pltpu
from jax.sharding import PartitionSpec as P

HSIZE = 32
LANES = 128
PENALTY = 6.0
F32 = jnp.float32
BF16 = jnp.bfloat16


def iota(shape, dim):
    return lax.broadcasted_iota(jnp.int32, shape, dim)


def split3(value):
    high = value.astype(BF16)
    rest = value - high.astype(F32)
    mid = rest.astype(BF16)
    low = (rest - mid.astype(F32)).astype(BF16)
    return high, mid, low


def same_head(rows):
    row = lax.rem(iota((rows, LANES), 0), LANES)
    return (row // HSIZE == iota((rows, LANES), 1) // HSIZE).astype(BF16)


def dot(a, b):
    return jnp.dot(a, b, preferred_element_type=F32)


def encoding_rows(days, dates, width):
    row, chan = iota((dates, width), 0), iota((dates, width), 1)
    even = lax.rem(chan, 2) == 0
    expo = (chan - lax.rem(chan, 2)).astype(F32) * F32(math.log(1000.0) / width)
    day = jnp.zeros((dates, width), F32)
    for t in range(dates):
        day = jnp.where(row == t, days[t].astype(F32), day)
    angle = day * jnp.exp(-expo)
    return jnp.where(even, jnp.sin(angle), jnp.cos(angle))


def fold_dates(value, join):
    pixels, dates, lanes = value.shape
    value = functools.reduce(join, [value[:, t : t + 8] for t in range(0, dates, 8)])
    for step in (1, 2, 4):
        value = value.reshape(-1, 2, 8, lanes)
        first, second = value[:, 0], value[:, 1]
        low = (iota(first.shape, 1) & step) == 0
        value = join(
            jnp.where(low, first, second),
            pltpu.roll(jnp.where(low, second, first), 8 - step, 1),
        )
    return value.reshape(pixels, lanes)


def attend_kernel(
    pixels, dates, tokens_hbm, mask_hbm, days_hbm, query_hbm, keyw_hbm, valw_hbm, out,
    tokens, mask, days, query, keyw, weights, sems, token_sems,
):
    tiles, width = tokens.shape[0], tokens.shape[-1]
    date = lax.axis_index("date")
    columns = pl.ds(3 * LANES, LANES)
    small = [
        pltpu.make_async_copy(days_hbm, days, sems.at[0]),
        pltpu.make_async_copy(query_hbm, query, sems.at[1]),
        pltpu.make_async_copy(keyw_hbm, keyw, sems.at[2]),
        pltpu.make_async_copy(valw_hbm, weights.at[:, columns], sems.at[3]),
        pltpu.make_async_copy(mask_hbm, mask, sems.at[4]),
    ]
    for copy in small:
        copy.start()
    loads = lambda i: pltpu.make_async_copy(tokens_hbm.at[date ^ i], tokens.at[i], token_sems.at[i])
    for i in range(tiles):
        loads(i).start()
    small[0].wait()
    table = encoding_rows(days, dates, width)
    small[1].wait()
    small[2].wait()
    scaled = keyw[...].astype(F32) * (query[...] * F32(HSIZE**-0.5))
    spread = same_head(LANES)
    high, mid, low = split3(scaled)
    folded = dot(high, spread) + (dot(mid, spread) + dot(low, spread))
    high, mid, low = split3(folded)
    weights[:, 0:LANES] = high
    weights[:, LANES : 2 * LANES] = mid
    weights[:, 2 * LANES : 3 * LANES] = low
    small[3].wait()
    small[4].wait()

    def one(i):
        feats = tokens[i].reshape(pixels, dates, width).astype(F32) + table[None]
        inputs = feats.astype(BF16).reshape(pixels * dates, width)
        both = dot(inputs, weights[...])
        score = both[:, 0:LANES] + (both[:, LANES : 2 * LANES] + both[:, 2 * LANES : 3 * LANES])
        vals = both[:, 3 * LANES : 4 * LANES]
        cloud = PENALTY * (1.0 - mask[date ^ i].astype(F32))
        score = score.reshape(pixels, dates, LANES) - lax.broadcast_in_dim(
            cloud, (pixels, dates, LANES), (0, 1)
        )
        top = jnp.max(score, axis=1)
        expo = jnp.exp(score - top[:, None, :])
        total = fold_dates(expo, jnp.add)
        summed = fold_dates(expo * vals.reshape(pixels, dates, LANES), jnp.add)
        part = (summed / total).astype(BF16)
        level = top + jnp.log(total)
        own = lax.rem(iota((pixels, LANES), 1), HSIZE) == iota((pixels, LANES), 0)
        packed = jnp.sum(jnp.where(own, level, 0.0), axis=0, keepdims=True)
        high, mid, low = split3(packed)
        row = iota((16, LANES), 0)
        tail = jnp.where(
            row == 0,
            high.astype(F32),
            jnp.where(row == 1, mid.astype(F32), jnp.where(row == 2, low.astype(F32), 0.0)),
        ).astype(BF16)
        out[i, 0:pixels, :] = part
        out[i, pixels : pixels + 16, :] = tail

    for i in range(tiles):
        loads(i).wait()
    if tiles <= 4:
        for i in range(tiles):
            one(i)
    else:
        pl.loop(0, tiles)(one)


def attend(tokens, cloud_mask, day_of_year, query, key_weight, value_weight):
    tiles, rows, cols, dates, width = tokens.shape
    pixels = rows * cols
    tokens = tokens.reshape(tiles, pixels * dates, width)
    mask = cloud_mask.reshape(tiles, pixels, dates)
    return pl.pallas_call(
        functools.partial(attend_kernel, pixels, dates),
        in_specs=[pl.BlockSpec(memory_space=pltpu.HBM)] * 6,
        out_specs=pl.BlockSpec(memory_space=pltpu.VMEM),
        out_shape=pltpu.VMEM((tiles, pixels + 16, LANES), BF16),
        scratch_shapes=[
            pltpu.VMEM(tokens.shape, BF16),
            pltpu.VMEM(mask.shape, jnp.int32),
            pltpu.SMEM(day_of_year.shape, jnp.int32),
            pltpu.VMEM((1, LANES), F32),
            pltpu.VMEM((width, LANES), BF16),
            pltpu.VMEM((width, 4 * LANES), BF16),
            pltpu.SemaphoreType.DMA((5,)),
            pltpu.SemaphoreType.DMA((tiles,)),
        ],
        compiler_params=pltpu.CompilerParams(vmem_limit_bytes=60 * 2**20),
    )(tokens, mask, day_of_year, query.reshape(1, LANES), key_weight, value_weight)


def merge(blocks, pixels, first, count):
    levels = [jnp.sum(tail.astype(F32), axis=0, keepdims=True) for _, tail in blocks]
    best = functools.reduce(jnp.maximum, levels)
    shares = [jnp.exp(level - best) for level in levels]
    total = functools.reduce(jnp.add, shares)
    own = lax.rem(iota((count, LANES), 1), HSIZE) == iota((count, LANES), 0) + first
    spread = same_head(2 * LANES)
    pooled = jnp.zeros((count, LANES), F32)
    for (part, _), share in zip(blocks, shares):
        share = share / total
        high = share.astype(BF16).astype(F32)
        both = jnp.concatenate([jnp.where(own, high, 0.0), jnp.where(own, share - high, 0.0)], axis=1)
        pooled = pooled + dot(both.astype(BF16), spread) * part.astype(F32)
    return pooled.astype(BF16).astype(F32)


def columns(field, cols):
    count = field.shape[0]
    col = lax.rem(iota(field.shape, 0), cols)
    left = jnp.where(col == 0, 0.0, pltpu.roll(field, 1, 0))
    right = jnp.where(col == cols - 1, 0.0, pltpu.roll(field, count - 1, 0))
    return jnp.concatenate([left, field, right], axis=1).astype(BF16)


def stencil(field, kernel, cols):
    count = field.shape[0] - 2 * cols
    return sum(dot(field, kernel[a])[a * cols : a * cols + count] for a in range(3))


def convolve_kernel(pixels, cols, slabs, slots, mine, theirs, got, swapped, first, other, second, out):
    dates = mine.shape[0]
    slab, head = lax.axis_index("tile"), lax.axis_index("head")
    odd = lax.rem(slab, 2) == 1
    halo = 2 * cols

    def in_order(own, partner):
        return jnp.concatenate(
            [jnp.where(head == 0, own, partner), jnp.where(head == 0, partner, own)], axis=1
        )

    starts, size = positions(dates)

    def block(core, slot, k, half, start, count):
        if k == 0:
            core = half
        place = slot * size + starts[k] + ((half if core == 0 else 1 - half) if k > 0 else 0)
        return tuple(
            jnp.where(head == core, got[place, rows], swapped[place, rows])
            for rows in (pl.ds(start, count), pl.ds(pixels, 16))
        )

    def kept(half):
        return tuple(
            jnp.where(head == half, mine[0, rows], theirs[0, rows])
            for rows in (pl.ds(0, pixels), pl.ds(pixels, 16))
        )

    centre = jnp.concatenate(
        [
            merge([kept(half)] + [block(0, 0, k, half, 0, pixels) for k in range(1, dates)], pixels, 0, pixels)
            for half in range(2)
        ],
        axis=1,
    )

    def neighbour(slot):
        above = odd if slot == 0 else jnp.logical_not(odd)
        start = pl.multiple_of(jnp.where(above, pixels - halo, 0), 16)
        return jnp.concatenate(
            [
                merge([block(1, slot, k, half, start, halo) for k in range(dates)], pixels, start, halo)
                for half in range(2)
            ],
            axis=1,
        )

    one = neighbour(0)
    two = neighbour(1) if slots > 1 else one
    above = jnp.where(slab > 0, jnp.where(odd, one, two), 0.0)
    below = jnp.where(slab < slabs - 1, jnp.where(odd, two, one), 0.0)
    field = jnp.concatenate([above, centre, below], axis=0)
    wide = columns(field, cols)
    hidden = in_order(stencil(wide, first, cols), stencil(wide, other, cols))
    count = pixels + 2 * cols
    row = iota(hidden.shape, 0)
    inside = jnp.logical_and(
        jnp.logical_or(row >= cols, slab > 0), jnp.logical_or(row < count - cols, slab < slabs - 1)
    )
    hidden = jnp.where(inside, jnp.maximum(hidden, 0.0), 0.0).astype(BF16).astype(F32)
    out[...] = stencil(columns(hidden, cols), second, cols).astype(BF16)


def convolve(mine, theirs, got, swapped, first, other, second, pixels, cols, slabs, slots):
    return pl.pallas_call(
        functools.partial(convolve_kernel, pixels, cols, slabs, slots),
        in_specs=[pl.BlockSpec(memory_space=pltpu.VMEM)] * 7,
        out_specs=pl.BlockSpec(memory_space=pltpu.VMEM),
        out_shape=jax.ShapeDtypeStruct((pixels, second.shape[-1]), BF16),
        compiler_params=pltpu.CompilerParams(vmem_limit_bytes=32 * 2**20),
    )(mine, theirs, got, swapped, first, other, second)


def arrangement(dates):
    return list(range(dates - 1, -1, -1))


def positions(dates):
    starts, size = {}, 0
    for k in arrangement(dates):
        starts[k] = size
        size += 2 if k > 0 else 1
    return starts, size


def routes(dates, slabs, k, slot):
    place = lambda d, t, core: (d * slabs + t) * 2 + core
    pairs = []
    for d in range(dates):
        for t in range(slabs):
            near = t ^ 1 if slot == 0 else ((t + 1) ^ 1) - 1
            if k > 0 and slot == 0:
                pairs.append((place(d, t, 0), place(d ^ k, t, 0)))
            if k == 0 and 0 <= near < slabs:
                pairs.append((place(d, t, 0), place(d, near, 0)))
            if 0 <= near < slabs:
                pairs.append((place(d, t, 1), place(d ^ k, near, 1)))
    return pairs


def local(slabs, tokens, cloud_mask, day_of_year, query, key_weight, value_weight, conv_first, conv_second):
    tiles, rows, cols, dates, width = tokens.shape
    pixels = rows * cols
    slots = 1 if slabs <= 2 else 2
    swap = [(0, 1), (1, 0)]
    first = conv_first.reshape(3, 3 * width, -1)
    second = conv_second.reshape(3, 3 * width, -1)
    other = lax.ppermute(first, "head", swap)
    mine = attend(tokens, cloud_mask, day_of_year, query, key_weight, value_weight)
    theirs = lax.ppermute(mine, "head", swap)
    pieces = []
    for slot in range(slots):
        for k in arrangement(tiles):
            block = jnp.stack([mine[k], theirs[k]]) if k > 0 else mine[:1]
            pieces.append(
                lax.ppermute(block, ("date", "tile", "head"), routes(tiles, slabs, k, slot))
            )
    got = jnp.concatenate(pieces)
    swapped = lax.ppermute(got, "head", swap)
    out = convolve(mine, theirs, got, swapped, first, other, second, pixels, cols, slabs, slots)
    return out.reshape(1, rows, cols, -1)


def solution(mesh):
    in_specs = (
        P("groups", "tile", None, "date", None),
        P("groups", "tile", None, "date"),
        P(("groups", "date")),
        P("head"),
        P(None, "head"),
        P(None, "head"),
        P(None, None, None, "head"),
        P(None, None, None, "head"),
    )
    out_specs = P(("groups", "date"), "tile", None, "head")
    body = functools.partial(local, mesh.shape["tile"])
    return jax.shard_map(body, mesh=mesh, in_specs=in_specs, out_specs=out_specs, check_vma=False)
```

```python
import functools
import math

import jax
import jax.numpy as jnp
from jax import lax
from jax.experimental import pallas as pl
from jax.experimental.pallas import tpu as pltpu
from jax.sharding import PartitionSpec as P

HSIZE = 32
LANES = 128
PENALTY = 6.0
LOG2E = math.log2(math.e)
F32 = jnp.float32
BF16 = jnp.bfloat16


def iota(shape, dim):
    return lax.broadcasted_iota(jnp.int32, shape, dim)


def split3(value):
    high = value.astype(BF16)
    rest = value - high.astype(F32)
    mid = rest.astype(BF16)
    low = (rest - mid.astype(F32)).astype(BF16)
    return high, mid, low


def same_head(rows):
    row = lax.rem(iota((rows, LANES), 0), LANES)
    return (row // HSIZE == iota((rows, LANES), 1) // HSIZE).astype(BF16)


def dot(a, b):
    return jnp.dot(a, b, preferred_element_type=F32)


def encoding_rows(days, dates, width):
    row, chan = iota((dates, width), 0), iota((dates, width), 1)
    even = lax.rem(chan, 2) == 0
    expo = (chan - lax.rem(chan, 2)).astype(F32) * F32(math.log(1000.0) / width)
    day = jnp.zeros((dates, width), F32)
    for t in range(dates):
        day = jnp.where(row == t, days[t].astype(F32), day)
    angle = day * jnp.exp(-expo)
    return jnp.where(even, jnp.sin(angle), jnp.cos(angle))


def fold_dates(value, join):
    pixels, dates, lanes = value.shape
    value = functools.reduce(join, [value[:, t : t + 8] for t in range(0, dates, 8)])
    for step in (1, 2, 4):
        value = value.reshape(-1, 2, 8, lanes)
        first, second = value[:, 0], value[:, 1]
        low = (iota(first.shape, 1) & step) == 0
        value = join(
            jnp.where(low, first, second),
            pltpu.roll(jnp.where(low, second, first), 8 - step, 1),
        )
    return value.reshape(pixels, lanes)


def pool(feats, table, weights, clear):
    pixels, dates = clear.shape
    width = feats.shape[-1]
    feats = feats.reshape(pixels, dates, width).astype(F32) + table[None]
    both = dot(feats.astype(BF16).reshape(pixels * dates, width), weights)
    score = both[:, 0:LANES] + (both[:, LANES : 2 * LANES] + both[:, 2 * LANES : 3 * LANES])
    vals = both[:, 3 * LANES : 4 * LANES].reshape(pixels, dates, LANES)
    cloud = F32(PENALTY * LOG2E) * (1.0 - clear.astype(F32))
    score = score.reshape(pixels, dates, LANES) - lax.broadcast_in_dim(
        cloud, (pixels, dates, LANES), (0, 1)
    )
    top = jnp.max(score, axis=1)
    expo = jnp.exp2(score - top[:, None, :])
    total = fold_dates(expo, jnp.add)
    summed = fold_dates(expo * vals, jnp.add)
    level = top + jnp.log(total) * F32(LOG2E)
    own = lax.rem(iota((pixels, LANES), 1), HSIZE) == iota((pixels, LANES), 0)
    packed = jnp.sum(jnp.where(own, level, 0.0), axis=0, keepdims=True)
    row = iota((16, LANES), 0)
    tail = jnp.zeros((16, LANES), F32)
    for place, piece in enumerate(split3(packed)):
        tail = jnp.where(row == place, piece.astype(F32), tail)
    return (summed / total).astype(BF16), tail.astype(BF16)


def pool_all(count, out, tokens, table, weights, clear):
    def one(i):
        part, tail = pool(tokens[i], table[...], weights[...], clear(i))
        pixels = part.shape[0]
        out[i, 0:pixels, :] = part
        out[i, pixels : pixels + 16, :] = tail

    if count <= 4:
        for i in range(count):
            one(i)
    else:
        pl.loop(0, count)(one)


def attend_kernel(
    dates, tokens_hbm, mask_hbm, days_hbm, query_hbm, keyw_hbm, valw_hbm, out,
    tokens, mask, weights, table, days, query, keyw, sems, token_sems,
):
    tiles, width = tokens.shape[0], tokens.shape[-1]
    date = lax.axis_index("date")
    columns = pl.ds(3 * LANES, LANES)
    small = [
        pltpu.make_async_copy(days_hbm, days, sems.at[0]),
        pltpu.make_async_copy(query_hbm, query, sems.at[1]),
        pltpu.make_async_copy(keyw_hbm, keyw, sems.at[2]),
        pltpu.make_async_copy(valw_hbm, weights.at[:, columns], sems.at[3]),
        pltpu.make_async_copy(mask_hbm, mask, sems.at[4]),
    ]
    for copy in small:
        copy.start()
    loads = [
        pltpu.make_async_copy(tokens_hbm.at[date ^ i], tokens.at[i], token_sems.at[i]) for i in range(tiles)
    ]
    for copy in loads:
        copy.start()
    small[0].wait()
    table[...] = encoding_rows(days, dates, width)
    small[1].wait()
    small[2].wait()
    scaled = keyw[...].astype(F32) * (query[...] * F32(HSIZE**-0.5 * LOG2E))
    spread = same_head(LANES)
    high, mid, low = split3(scaled)
    folded = dot(high, spread) + (dot(mid, spread) + dot(low, spread))
    for place, piece in enumerate(split3(folded)):
        weights[:, place * LANES : (place + 1) * LANES] = piece
    small[3].wait()
    small[4].wait()
    for copy in loads:
        copy.wait()
    pool_all(tiles, out, tokens, table, weights, lambda i: mask[date ^ i])


def attend(tokens, cloud_mask, day_of_year, query, key_weight, value_weight):
    tiles, rows, cols, dates, width = tokens.shape
    pixels = rows * cols
    tokens = tokens.reshape(tiles, pixels * dates, width)
    mask = cloud_mask.reshape(tiles, pixels, dates)
    return pl.pallas_call(
        functools.partial(attend_kernel, dates),
        in_specs=[pl.BlockSpec(memory_space=pltpu.HBM)] * 6,
        out_specs=pl.BlockSpec(memory_space=pltpu.VMEM),
        out_shape=pltpu.VMEM((tiles, pixels + 16, LANES), BF16),
        scratch_shapes=[
            pltpu.VMEM(tokens.shape, BF16),
            pltpu.VMEM(mask.shape, jnp.int32),
            pltpu.VMEM((width, 4 * LANES), BF16),
            pltpu.VMEM((dates, width), F32),
            pltpu.SMEM(day_of_year.shape, jnp.int32),
            pltpu.VMEM((1, LANES), F32),
            pltpu.VMEM((width, LANES), BF16),
            pltpu.SemaphoreType.DMA((5,)),
            pltpu.SemaphoreType.DMA((tiles,)),
        ],
        compiler_params=pltpu.CompilerParams(vmem_limit_bytes=60 * 2**20),
    )(tokens, mask, day_of_year, query.reshape(1, LANES), key_weight, value_weight)


def merge(blocks, pixels, start, count):
    levels = [jnp.sum(tail.astype(F32), axis=0, keepdims=True) for _, tail in blocks]
    best = functools.reduce(jnp.maximum, levels)
    shares = [jnp.exp2(level - best) for level in levels]
    scale = 1.0 / functools.reduce(jnp.add, shares)
    own = lax.rem(iota((count, LANES), 1), HSIZE) == iota((count, LANES), 0) + start
    spread = same_head(2 * LANES)
    pooled = jnp.zeros((count, LANES), F32)
    for (part, _), share in zip(blocks, shares):
        share = share * scale
        high = share.astype(BF16).astype(F32)
        both = jnp.concatenate([jnp.where(own, high, 0.0), jnp.where(own, share - high, 0.0)], axis=1)
        pooled = pooled + dot(both.astype(BF16), spread) * part.astype(F32)
    return pooled.astype(BF16).astype(F32)


def columns(field, cols):
    count = field.shape[0]
    col = lax.rem(iota(field.shape, 0), cols)
    left = jnp.where(col == 0, 0.0, pltpu.roll(field, 1, 0))
    right = jnp.where(col == cols - 1, 0.0, pltpu.roll(field, count - 1, 0))
    return jnp.concatenate([left, field, right], axis=1).astype(BF16)


def stencil(field, kernel, cols):
    count = field.shape[0] - 2 * cols
    return sum(dot(field, kernel[a])[a * cols : a * cols + count] for a in range(3))


def convolve_kernel(pixels, cols, slabs, slots, mine, theirs, got, swapped, first, other, second, out):
    dates = mine.shape[0]
    slab, head = lax.axis_index("tile"), lax.axis_index("head")
    odd = lax.rem(slab, 2) == 1
    halo = 2 * cols

    def in_order(own, partner):
        return jnp.concatenate(
            [jnp.where(head == 0, own, partner), jnp.where(head == 0, partner, own)], axis=1
        )

    starts = positions(dates, slots)

    def block(core, slot, k, half, start, count):
        direct = (slot, k, "halo" if core else "own")
        if direct in starts:
            place, core = starts[direct], half
        else:
            place = starts[slot, k, "both"] + (1 - half if core else half)
        return tuple(
            jnp.where(head == core, got[place, rows], swapped[place, rows])
            for rows in (pl.ds(start, count), pl.ds(pixels, 16))
        )

    def kept(half):
        return tuple(
            jnp.where(head == half, mine[0, rows], theirs[0, rows])
            for rows in (pl.ds(0, pixels), pl.ds(pixels, 16))
        )

    centre = jnp.concatenate(
        [
            merge([kept(half)] + [block(0, 0, k, half, 0, pixels) for k in range(1, dates)], pixels, 0, pixels)
            for half in range(2)
        ],
        axis=1,
    )

    def neighbour(slot):
        up = odd if slot == 0 else jnp.logical_not(odd)
        start = pl.multiple_of(jnp.where(up, pixels - halo, 0), 16)
        return jnp.concatenate(
            [
                merge([block(1, slot, k, half, start, halo) for k in range(dates)], pixels, start, halo)
                for half in range(2)
            ],
            axis=1,
        )

    one = neighbour(0)
    two = neighbour(1) if slots > 1 else one
    above = jnp.where(slab > 0, jnp.where(odd, one, two), 0.0)
    below = jnp.where(slab < slabs - 1, jnp.where(odd, two, one), 0.0)
    field = jnp.concatenate([above, centre, below], axis=0)
    wide = columns(field, cols)
    hidden = in_order(stencil(wide, first, cols), stencil(wide, other, cols))
    count = pixels + 2 * cols
    row = iota(hidden.shape, 0)
    inside = jnp.logical_and(
        jnp.logical_or(row >= cols, slab > 0), jnp.logical_or(row < count - cols, slab < slabs - 1)
    )
    hidden = jnp.where(inside, jnp.maximum(hidden, 0.0), 0.0).astype(BF16).astype(F32)
    out[...] = stencil(columns(hidden, cols), second, cols).astype(BF16)


def convolve(mine, theirs, got, swapped, first, other, second, pixels, cols, slabs, slots):
    return pl.pallas_call(
        functools.partial(convolve_kernel, pixels, cols, slabs, slots),
        in_specs=[pl.BlockSpec(memory_space=pltpu.VMEM)] * 7,
        out_specs=pl.BlockSpec(memory_space=pltpu.VMEM),
        out_shape=jax.ShapeDtypeStruct((pixels, second.shape[-1]), BF16),
        compiler_params=pltpu.CompilerParams(vmem_limit_bytes=32 * 2**20),
    )(mine, theirs, got, swapped, first, other, second)


def messages(dates, slots):
    found = []
    for slot in range(slots):
        for k in list(range(dates // 2, dates)) + list(range(dates // 2 - 1, -1, -1)):
            if k in (0,):
                found += [(slot, k, "own")] if k > 0 and slot == 0 else []
                found.append((slot, k, "halo"))
            else:
                found.append((slot, k, "both"))
    return found


def positions(dates, slots):
    starts, size = {}, 0
    for message in messages(dates, slots):
        starts[message] = size
        size += 2 if message[2] == "both" else 1
    return starts


def routes(dates, slabs, slot, k, kind):
    place = lambda d, t, core: (d * slabs + t) * 2 + core
    pairs = []
    for d in range(dates):
        for t in range(slabs):
            near = t ^ 1 if slot == 0 else ((t + 1) ^ 1) - 1
            for core in range(2):
                own = kind == "own" or (kind == "both" and core == 0)
                if own and slot == 0:
                    pairs.append((place(d, t, core), place(d ^ k, t, core)))
                if not own and 0 <= near < slabs:
                    pairs.append((place(d, t, core), place(d ^ k, near, core)))
    return pairs


def local(slabs, tokens, cloud_mask, day_of_year, query, key_weight, value_weight, conv_first, conv_second):
    tiles, rows, cols, dates, width = tokens.shape
    pixels = rows * cols
    slots = 1 if slabs <= 2 else 2
    swap = [(0, 1), (1, 0)]
    first = conv_first.reshape(3, 3 * width, -1)
    second = conv_second.reshape(3, 3 * width, -1)
    other = lax.ppermute(first, "head", swap)
    mine = attend(tokens, cloud_mask, day_of_year, query, key_weight, value_weight)
    theirs = lax.ppermute(mine, "head", swap)
    pieces = []
    for slot, k, kind in messages(tiles, slots):
        block = jnp.stack([mine[k], theirs[k]]) if kind == "both" else mine[k : k + 1]
        pairs = routes(tiles, slabs, slot, k, kind)
        pieces.append(lax.ppermute(block, ("date", "tile", "head"), pairs))
    got = jnp.concatenate(pieces)
    swapped = lax.ppermute(got, "head", swap)
    out = convolve(mine, theirs, got, swapped, first, other, second, pixels, cols, slabs, slots)
    return out.reshape(1, rows, cols, -1)


def solution(mesh):
    in_specs = (
        P("groups", "tile", None, "date", None),
        P("groups", "tile", None, "date"),
        P(("groups", "date")),
        P("head"),
        P(None, "head"),
        P(None, "head"),
        P(None, None, None, "head"),
        P(None, None, None, "head"),
    )
    out_specs = P(("groups", "date"), "tile", None, "head")
    body = functools.partial(local, mesh.shape["tile"])
    return jax.shard_map(body, mesh=mesh, in_specs=in_specs, out_specs=out_specs, check_vma=False)
```

```python
import functools
import math

import jax
import jax.numpy as jnp
from jax import lax
from jax.experimental import pallas as pl
from jax.experimental.pallas import tpu as pltpu
from jax.sharding import PartitionSpec as P

HSIZE = 32
LANES = 128
PENALTY = 6.0
LOG2E = math.log2(math.e)
F32 = jnp.float32
BF16 = jnp.bfloat16


def along(d, k, dates):
    if dates & (dates - 1):
        return (d + k) % dates
    rank, shift = d, 1
    while shift < dates:
        rank, shift = rank ^ (rank >> shift), 2 * shift
    rank = (rank + k) & (dates - 1)
    return rank ^ (rank >> 1)


def iota(shape, dim):
    return lax.broadcasted_iota(jnp.int32, shape, dim)


def split3(value):
    high = value.astype(BF16)
    rest = value - high.astype(F32)
    mid = rest.astype(BF16)
    low = (rest - mid.astype(F32)).astype(BF16)
    return high, mid, low


def same_head(rows):
    row = lax.rem(iota((rows, LANES), 0), LANES)
    return (row // HSIZE == iota((rows, LANES), 1) // HSIZE).astype(BF16)


def dot(a, b):
    return jnp.dot(a, b, preferred_element_type=F32)


def encoding_rows(days, dates, width):
    row, chan = iota((dates, width), 0), iota((dates, width), 1)
    even = lax.rem(chan, 2) == 0
    expo = (chan - lax.rem(chan, 2)).astype(F32) * F32(math.log(1000.0) / width)
    day = jnp.zeros((dates, width), F32)
    for t in range(dates):
        day = jnp.where(row == t, days[t].astype(F32), day)
    angle = day * jnp.exp(-expo)
    return jnp.where(even, jnp.sin(angle), jnp.cos(angle))


def fold_dates(value, join):
    pixels, dates, lanes = value.shape
    value = functools.reduce(join, [value[:, t : t + 8] for t in range(0, dates, 8)])
    for step in (1, 2, 4):
        value = value.reshape(-1, 2, 8, lanes)
        first, second = value[:, 0], value[:, 1]
        low = (iota(first.shape, 1) & step) == 0
        value = join(
            jnp.where(low, first, second),
            pltpu.roll(jnp.where(low, second, first), 8 - step, 1),
        )
    return value.reshape(pixels, lanes)


def pool(feats, table, weights, clear):
    pixels, dates = clear.shape
    width = feats.shape[-1]
    feats = feats.reshape(pixels, dates, width).astype(F32) + table[None]
    both = dot(feats.astype(BF16).reshape(pixels * dates, width), weights)
    score = both[:, 0:LANES] + (both[:, LANES : 2 * LANES] + both[:, 2 * LANES : 3 * LANES])
    vals = both[:, 3 * LANES : 4 * LANES].reshape(pixels, dates, LANES)
    cloud = F32(PENALTY * LOG2E) * (1.0 - clear.astype(F32))
    score = score.reshape(pixels, dates, LANES) - lax.broadcast_in_dim(
        cloud, (pixels, dates, LANES), (0, 1)
    )
    top = jnp.max(score, axis=1)
    expo = jnp.exp2(score - top[:, None, :])
    total = fold_dates(expo, jnp.add)
    summed = fold_dates(expo * vals, jnp.add)
    level = top + jnp.log(total) * F32(LOG2E)
    own = lax.rem(iota((pixels, LANES), 1), HSIZE) == iota((pixels, LANES), 0)
    packed = jnp.sum(jnp.where(own, level, 0.0), axis=0, keepdims=True)
    row = iota((16, LANES), 0)
    tail = jnp.zeros((16, LANES), F32)
    for place, piece in enumerate(split3(packed)):
        tail = jnp.where(row == place, piece.astype(F32), tail)
    return (summed / total).astype(BF16), tail.astype(BF16)


def pool_all(count, out, tokens, table, weights, clear):
    def one(i):
        part, tail = pool(tokens[i], table[...], weights[...], clear(i))
        pixels = part.shape[0]
        out[i, 0:pixels, :] = part
        out[i, pixels : pixels + 16, :] = tail

    if count <= 4:
        for i in range(count):
            one(i)
    else:
        pl.loop(0, count)(one)


def attend_kernel(
    dates, tokens_hbm, mask_hbm, days_hbm, query_hbm, keyw_hbm, valw_hbm, out,
    tokens, mask, weights, table, days, query, keyw, sems, token_sems,
):
    tiles, width = tokens.shape[0], tokens.shape[-1]
    date = lax.axis_index("date")
    columns = pl.ds(3 * LANES, LANES)
    small = [
        pltpu.make_async_copy(days_hbm, days, sems.at[0]),
        pltpu.make_async_copy(query_hbm, query, sems.at[1]),
        pltpu.make_async_copy(keyw_hbm, keyw, sems.at[2]),
        pltpu.make_async_copy(valw_hbm, weights.at[:, columns], sems.at[3]),
        pltpu.make_async_copy(mask_hbm, mask, sems.at[4]),
    ]
    for copy in small:
        copy.start()
    loads = [
        pltpu.make_async_copy(tokens_hbm.at[along(date, i, tiles)], tokens.at[i], token_sems.at[i]) for i in range(tiles)
    ]
    for copy in loads:
        copy.start()
    small[0].wait()
    table[...] = encoding_rows(days, dates, width)
    small[1].wait()
    small[2].wait()
    scaled = keyw[...].astype(F32) * (query[...] * F32(HSIZE**-0.5 * LOG2E))
    spread = same_head(LANES)
    high, mid, low = split3(scaled)
    folded = dot(high, spread) + (dot(mid, spread) + dot(low, spread))
    for place, piece in enumerate(split3(folded)):
        weights[:, place * LANES : (place + 1) * LANES] = piece
    small[3].wait()
    small[4].wait()
    for copy in loads:
        copy.wait()
    pool_all(tiles, out, tokens, table, weights, lambda i: mask[along(date, i, tiles)])


def attend(tokens, cloud_mask, day_of_year, query, key_weight, value_weight):
    tiles, rows, cols, dates, width = tokens.shape
    pixels = rows * cols
    tokens = tokens.reshape(tiles, pixels * dates, width)
    mask = cloud_mask.reshape(tiles, pixels, dates)
    return pl.pallas_call(
        functools.partial(attend_kernel, dates),
        in_specs=[pl.BlockSpec(memory_space=pltpu.HBM)] * 6,
        out_specs=pl.BlockSpec(memory_space=pltpu.VMEM),
        out_shape=pltpu.VMEM((tiles, pixels + 16, LANES), BF16),
        scratch_shapes=[
            pltpu.VMEM(tokens.shape, BF16),
            pltpu.VMEM(mask.shape, jnp.int32),
            pltpu.VMEM((width, 4 * LANES), BF16),
            pltpu.VMEM((dates, width), F32),
            pltpu.SMEM(day_of_year.shape, jnp.int32),
            pltpu.VMEM((1, LANES), F32),
            pltpu.VMEM((width, LANES), BF16),
            pltpu.SemaphoreType.DMA((5,)),
            pltpu.SemaphoreType.DMA((tiles,)),
        ],
        compiler_params=pltpu.CompilerParams(vmem_limit_bytes=60 * 2**20),
    )(tokens, mask, day_of_year, query.reshape(1, LANES), key_weight, value_weight)


def merge(blocks, pixels, start, count):
    levels = [jnp.sum(tail.astype(F32), axis=0, keepdims=True) for _, tail in blocks]
    best = functools.reduce(jnp.maximum, levels)
    shares = [jnp.exp2(level - best) for level in levels]
    scale = 1.0 / functools.reduce(jnp.add, shares)
    own = lax.rem(iota((count, LANES), 1), HSIZE) == iota((count, LANES), 0) + start
    spread = same_head(2 * LANES)
    pooled = jnp.zeros((count, LANES), F32)
    for (part, _), share in zip(blocks, shares):
        share = share * scale
        high = share.astype(BF16).astype(F32)
        both = jnp.concatenate([jnp.where(own, high, 0.0), jnp.where(own, share - high, 0.0)], axis=1)
        pooled = pooled + dot(both.astype(BF16), spread) * part.astype(F32)
    return pooled.astype(BF16).astype(F32)


def columns(field, cols):
    count = field.shape[0]
    col = lax.rem(iota(field.shape, 0), cols)
    left = jnp.where(col == 0, 0.0, pltpu.roll(field, 1, 0))
    right = jnp.where(col == cols - 1, 0.0, pltpu.roll(field, count - 1, 0))
    return jnp.concatenate([left, field, right], axis=1).astype(BF16)


def stencil(field, kernel, cols):
    count = field.shape[0] - 2 * cols
    return sum(dot(field, kernel[a])[a * cols : a * cols + count] for a in range(3))


def convolve_kernel(pixels, cols, slabs, slots, mine, theirs, got, swapped, first, other, second, out):
    dates = mine.shape[0]
    slab, head = lax.axis_index("tile"), lax.axis_index("head")
    odd = lax.rem(slab, 2) == 1
    halo = 2 * cols

    def in_order(own, partner):
        return jnp.concatenate(
            [jnp.where(head == 0, own, partner), jnp.where(head == 0, partner, own)], axis=1
        )

    starts = positions(dates, slots)

    def block(core, slot, k, half, start, count):
        place = starts[slot, k]
        if k > 0:
            place += 1 - half if core else half
        else:
            core = half
        return tuple(
            jnp.where(head == core, got[place, rows], swapped[place, rows])
            for rows in (pl.ds(start, count), pl.ds(pixels, 16))
        )

    def kept(half):
        return tuple(
            jnp.where(head == half, mine[0, rows], theirs[0, rows])
            for rows in (pl.ds(0, pixels), pl.ds(pixels, 16))
        )

    centre = jnp.concatenate(
        [
            merge([kept(half)] + [block(0, 0, k, half, 0, pixels) for k in range(1, dates)], pixels, 0, pixels)
            for half in range(2)
        ],
        axis=1,
    )

    def neighbour(slot):
        up = odd if slot == 0 else jnp.logical_not(odd)
        start = pl.multiple_of(jnp.where(up, pixels - halo, 0), 16)
        return jnp.concatenate(
            [
                merge([block(1, slot, k, half, start, halo) for k in range(dates)], pixels, start, halo)
                for half in range(2)
            ],
            axis=1,
        )

    one = neighbour(0)
    two = neighbour(1) if slots > 1 else one
    above = jnp.where(slab > 0, jnp.where(odd, one, two), 0.0)
    below = jnp.where(slab < slabs - 1, jnp.where(odd, two, one), 0.0)
    field = jnp.concatenate([above, centre, below], axis=0)
    wide = columns(field, cols)
    hidden = in_order(stencil(wide, first, cols), stencil(wide, other, cols))
    count = pixels + 2 * cols
    row = iota(hidden.shape, 0)
    inside = jnp.logical_and(
        jnp.logical_or(row >= cols, slab > 0), jnp.logical_or(row < count - cols, slab < slabs - 1)
    )
    hidden = jnp.where(inside, jnp.maximum(hidden, 0.0), 0.0).astype(BF16).astype(F32)
    out[...] = stencil(columns(hidden, cols), second, cols).astype(BF16)


def convolve(mine, theirs, got, swapped, first, other, second, pixels, cols, slabs, slots):
    return pl.pallas_call(
        functools.partial(convolve_kernel, pixels, cols, slabs, slots),
        in_specs=[pl.BlockSpec(memory_space=pltpu.VMEM)] * 7,
        out_specs=pl.BlockSpec(memory_space=pltpu.VMEM),
        out_shape=jax.ShapeDtypeStruct((pixels, second.shape[-1]), BF16),
        compiler_params=pltpu.CompilerParams(vmem_limit_bytes=32 * 2**20),
    )(mine, theirs, got, swapped, first, other, second)


def messages(dates, slots):
    return [(slot, k) for slot in range(slots) for k in list(range(1, dates)) + [0]]


def positions(dates, slots):
    starts, size = {}, 0
    for message in messages(dates, slots):
        starts[message] = size
        size += 2 if message[1] else 1
    return starts


def routes(dates, slabs, slot, k):
    place = lambda d, t, core: (d * slabs + t) * 2 + core
    pairs = []
    for d in range(dates):
        for t in range(slabs):
            near = t ^ 1 if slot == 0 else ((t + 1) ^ 1) - 1
            for core in range(2):
                own = k > 0 and core == 0
                if own and slot == 0:
                    pairs.append((place(d, t, core), place(along(d, k, dates), t, core)))
                if not own and 0 <= near < slabs:
                    pairs.append((place(d, t, core), place(along(d, k, dates), near, core)))
    return pairs


def local(slabs, tokens, cloud_mask, day_of_year, query, key_weight, value_weight, conv_first, conv_second):
    tiles, rows, cols, dates, width = tokens.shape
    pixels = rows * cols
    slots = 1 if slabs <= 2 else 2
    swap = [(0, 1), (1, 0)]
    first = conv_first.reshape(3, 3 * width, -1)
    second = conv_second.reshape(3, 3 * width, -1)
    other = lax.ppermute(first, "head", swap)
    mine = attend(tokens, cloud_mask, day_of_year, query, key_weight, value_weight)
    theirs = lax.ppermute(mine, "head", swap)
    pieces = []
    for slot, k in messages(tiles, slots):
        block = jnp.stack([mine[k], theirs[k]]) if k > 0 else mine[:1]
        pieces.append(lax.ppermute(block, ("date", "tile", "head"), routes(tiles, slabs, slot, k)))
    got = jnp.concatenate(pieces)
    swapped = lax.ppermute(got, "head", swap)
    out = convolve(mine, theirs, got, swapped, first, other, second, pixels, cols, slabs, slots)
    return out.reshape(1, rows, cols, -1)


def solution(mesh):
    in_specs = (
        P("groups", "tile", None, "date", None),
        P("groups", "tile", None, "date"),
        P(("groups", "date")),
        P("head"),
        P(None, "head"),
        P(None, "head"),
        P(None, None, None, "head"),
        P(None, None, None, "head"),
    )
    out_specs = P(("groups", "date"), "tile", None, "head")
    body = functools.partial(local, mesh.shape["tile"])
    return jax.shard_map(body, mesh=mesh, in_specs=in_specs, out_specs=out_specs, check_vma=False)
```

```python
import functools
import math

import jax
import jax.numpy as jnp
from jax import lax
from jax.experimental import pallas as pl
from jax.experimental.pallas import tpu as pltpu
from jax.sharding import PartitionSpec as P

HSIZE = 32
LANES = 128
PENALTY = 6.0
LOG2E = math.log2(math.e)
F32 = jnp.float32
BF16 = jnp.bfloat16


def along(d, k, dates):
    if dates & (dates - 1):
        return (d + k) % dates
    rank, shift = d, 1
    while shift < dates:
        rank, shift = rank ^ (rank >> shift), 2 * shift
    rank = (rank + k) & (dates - 1)
    return rank ^ (rank >> 1)


def iota(shape, dim):
    return lax.broadcasted_iota(jnp.int32, shape, dim)


def split3(value):
    high = value.astype(BF16)
    rest = value - high.astype(F32)
    mid = rest.astype(BF16)
    low = (rest - mid.astype(F32)).astype(BF16)
    return high, mid, low


def same_head(rows):
    row = lax.rem(iota((rows, LANES), 0), LANES)
    return (row // HSIZE == iota((rows, LANES), 1) // HSIZE).astype(BF16)


def dot(a, b):
    return jnp.dot(a, b, preferred_element_type=F32)


def encoding_rows(days, dates, width):
    row, chan = iota((dates, width), 0), iota((dates, width), 1)
    even = lax.rem(chan, 2) == 0
    expo = (chan - lax.rem(chan, 2)).astype(F32) * F32(math.log(1000.0) / width)
    day = jnp.zeros((dates, width), F32)
    for t in range(dates):
        day = jnp.where(row == t, days[t].astype(F32), day)
    angle = day * jnp.exp(-expo)
    return jnp.where(even, jnp.sin(angle), jnp.cos(angle))


def fold_dates(value, join):
    pixels, dates, lanes = value.shape
    value = functools.reduce(join, [value[:, t : t + 8] for t in range(0, dates, 8)])
    for step in (1, 2, 4):
        value = value.reshape(-1, 2, 8, lanes)
        first, second = value[:, 0], value[:, 1]
        low = (iota(first.shape, 1) & step) == 0
        value = join(
            jnp.where(low, first, second),
            pltpu.roll(jnp.where(low, second, first), 8 - step, 1),
        )
    return value.reshape(pixels, lanes)


def pool(feats, table, weights, clear):
    pixels, dates = clear.shape
    width = feats.shape[-1]
    feats = feats.reshape(pixels, dates, width).astype(F32) + table[None]
    both = dot(feats.astype(BF16).reshape(pixels * dates, width), weights)
    score = both[:, 0:LANES] + (both[:, LANES : 2 * LANES] + both[:, 2 * LANES : 3 * LANES])
    vals = both[:, 3 * LANES : 4 * LANES].reshape(pixels, dates, LANES)
    cloud = F32(PENALTY * LOG2E) * (1.0 - clear.astype(F32))
    score = score.reshape(pixels, dates, LANES) - lax.broadcast_in_dim(
        cloud, (pixels, dates, LANES), (0, 1)
    )
    top = jnp.max(score, axis=1)
    expo = jnp.exp2(score - top[:, None, :])
    total = fold_dates(expo, jnp.add)
    summed = fold_dates(expo * vals, jnp.add)
    level = top + jnp.log(total) * F32(LOG2E)
    own = lax.rem(iota((pixels, LANES), 1), HSIZE) == iota((pixels, LANES), 0)
    packed = jnp.sum(jnp.where(own, level, 0.0), axis=0, keepdims=True)
    row = iota((16, LANES), 0)
    tail = jnp.zeros((16, LANES), F32)
    for place, piece in enumerate(split3(packed)):
        tail = jnp.where(row == place, piece.astype(F32), tail)
    return (summed / total).astype(BF16), tail.astype(BF16)


def pool_all(count, out, tokens, table, weights, clear):
    def one(i):
        part, tail = pool(tokens[i], table[...], weights[...], clear(i))
        pixels = part.shape[0]
        out[i, 0:pixels, :] = part
        out[i, pixels : pixels + 16, :] = tail

    if count <= 4:
        for i in range(count):
            one(i)
    else:
        pl.loop(0, count)(one)


def attend_kernel(
    dates, tokens_hbm, mask_hbm, days_hbm, query_hbm, keyw_hbm, valw_hbm, out,
    tokens, mask, weights, table, days, query, keyw, sems, token_sems,
):
    tiles, width = tokens.shape[0], tokens.shape[-1]
    date = lax.axis_index("date")
    columns = pl.ds(3 * LANES, LANES)
    small = [
        pltpu.make_async_copy(days_hbm, days, sems.at[0]),
        pltpu.make_async_copy(query_hbm, query, sems.at[1]),
        pltpu.make_async_copy(keyw_hbm, keyw, sems.at[2]),
        pltpu.make_async_copy(valw_hbm, weights.at[:, columns], sems.at[3]),
        pltpu.make_async_copy(mask_hbm, mask, sems.at[4]),
    ]
    for copy in small:
        copy.start()
    loads = [
        pltpu.make_async_copy(tokens_hbm.at[along(date, i, tiles)], tokens.at[i], token_sems.at[i]) for i in range(tiles)
    ]
    for copy in loads:
        copy.start()
    small[0].wait()
    table[...] = encoding_rows(days, dates, width)
    small[1].wait()
    small[2].wait()
    scaled = keyw[...].astype(F32) * (query[...] * F32(HSIZE**-0.5 * LOG2E))
    spread = same_head(LANES)
    high, mid, low = split3(scaled)
    folded = dot(high, spread) + (dot(mid, spread) + dot(low, spread))
    for place, piece in enumerate(split3(folded)):
        weights[:, place * LANES : (place + 1) * LANES] = piece
    small[3].wait()
    small[4].wait()
    for copy in loads:
        copy.wait()
    pool_all(tiles, out, tokens, table, weights, lambda i: mask[along(date, i, tiles)])


def attend(tokens, cloud_mask, day_of_year, query, key_weight, value_weight):
    tiles, rows, cols, dates, width = tokens.shape
    pixels = rows * cols
    tokens = tokens.reshape(tiles, pixels * dates, width)
    mask = cloud_mask.reshape(tiles, pixels, dates)
    return pl.pallas_call(
        functools.partial(attend_kernel, dates),
        in_specs=[pl.BlockSpec(memory_space=pltpu.HBM)] * 6,
        out_specs=pl.BlockSpec(memory_space=pltpu.VMEM),
        out_shape=pltpu.VMEM((tiles, pixels + 16, LANES), BF16),
        scratch_shapes=[
            pltpu.VMEM(tokens.shape, BF16),
            pltpu.VMEM(mask.shape, jnp.int32),
            pltpu.VMEM((width, 4 * LANES), BF16),
            pltpu.VMEM((dates, width), F32),
            pltpu.SMEM(day_of_year.shape, jnp.int32),
            pltpu.VMEM((1, LANES), F32),
            pltpu.VMEM((width, LANES), BF16),
            pltpu.SemaphoreType.DMA((5,)),
            pltpu.SemaphoreType.DMA((tiles,)),
        ],
        compiler_params=pltpu.CompilerParams(vmem_limit_bytes=60 * 2**20),
    )(tokens, mask, day_of_year, query.reshape(1, LANES), key_weight, value_weight)


def merge(blocks, pixels, start, count):
    levels = [jnp.sum(tail.astype(F32), axis=0, keepdims=True) for _, tail in blocks]
    best = functools.reduce(jnp.maximum, levels)
    shares = [jnp.exp2(level - best) for level in levels]
    scale = 1.0 / functools.reduce(jnp.add, shares)
    own = lax.rem(iota((count, LANES), 1), HSIZE) == iota((count, LANES), 0) + start
    spread = same_head(2 * LANES)
    pooled = jnp.zeros((count, LANES), F32)
    for (part, _), share in zip(blocks, shares):
        share = share * scale
        high = share.astype(BF16).astype(F32)
        both = jnp.concatenate([jnp.where(own, high, 0.0), jnp.where(own, share - high, 0.0)], axis=1)
        pooled = pooled + dot(both.astype(BF16), spread) * part.astype(F32)
    return pooled.astype(BF16).astype(F32)


def columns(field, cols):
    count = field.shape[0]
    col = lax.rem(iota(field.shape, 0), cols)
    left = jnp.where(col == 0, 0.0, pltpu.roll(field, 1, 0))
    right = jnp.where(col == cols - 1, 0.0, pltpu.roll(field, count - 1, 0))
    return jnp.concatenate([left, field, right], axis=1).astype(BF16)


def stencil(field, kernel, cols):
    count = field.shape[0] - 2 * cols
    return sum(dot(field, kernel[a])[a * cols : a * cols + count] for a in range(3))


def convolve_kernel(pixels, cols, slabs, slots, mine, theirs, *refs):
    dates = mine.shape[0]
    slab, head = lax.axis_index("tile"), lax.axis_index("head")
    odd = lax.rem(slab, 2) == 1
    halo = 2 * cols

    def in_order(own, partner):
        return jnp.concatenate(
            [jnp.where(head == 0, own, partner), jnp.where(head == 0, partner, own)], axis=1
        )

    places = positions(dates, slots)
    parts = (len(refs) - 4) // 2
    got, swapped, (first, other, second, out) = refs[:parts], refs[parts:-4], refs[-4:]

    def block(core, slot, k, half, start, count):
        which, place = places[slot, k]
        if k > 0:
            place += 1 - half if core else half
        else:
            core = half
        return tuple(
            jnp.where(head == core, got[which][place, rows], swapped[which][place, rows])
            for rows in (pl.ds(start, count), pl.ds(pixels, 16))
        )

    def kept(half):
        return tuple(
            jnp.where(head == half, mine[0, rows], theirs[0, rows])
            for rows in (pl.ds(0, pixels), pl.ds(pixels, 16))
        )

    centre = jnp.concatenate(
        [
            merge([kept(half)] + [block(0, 0, k, half, 0, pixels) for k in range(1, dates)], pixels, 0, pixels)
            for half in range(2)
        ],
        axis=1,
    )

    def neighbour(slot):
        up = odd if slot == 0 else jnp.logical_not(odd)
        start = pl.multiple_of(jnp.where(up, pixels - halo, 0), 16)
        return jnp.concatenate(
            [
                merge([block(1, slot, k, half, start, halo) for k in range(dates)], pixels, start, halo)
                for half in range(2)
            ],
            axis=1,
        )

    one = neighbour(0)
    two = neighbour(1) if slots > 1 else one
    above = jnp.where(slab > 0, jnp.where(odd, one, two), 0.0)
    below = jnp.where(slab < slabs - 1, jnp.where(odd, two, one), 0.0)
    field = jnp.concatenate([above, centre, below], axis=0)
    wide = columns(field, cols)
    hidden = in_order(stencil(wide, first, cols), stencil(wide, other, cols))
    count = pixels + 2 * cols
    row = iota(hidden.shape, 0)
    inside = jnp.logical_and(
        jnp.logical_or(row >= cols, slab > 0), jnp.logical_or(row < count - cols, slab < slabs - 1)
    )
    hidden = jnp.where(inside, jnp.maximum(hidden, 0.0), 0.0).astype(BF16).astype(F32)
    out[...] = stencil(columns(hidden, cols), second, cols).astype(BF16)


def convolve(mine, theirs, got, swapped, first, other, second, pixels, cols, slabs, slots):
    return pl.pallas_call(
        functools.partial(convolve_kernel, pixels, cols, slabs, slots),
        in_specs=[pl.BlockSpec(memory_space=pltpu.VMEM)] * (5 + 2 * len(got)),
        out_specs=pl.BlockSpec(memory_space=pltpu.VMEM),
        out_shape=jax.ShapeDtypeStruct((pixels, second.shape[-1]), BF16),
        compiler_params=pltpu.CompilerParams(vmem_limit_bytes=32 * 2**20),
    )(mine, theirs, *got, *swapped, first, other, second)


def messages(dates, slots):
    return [(slot, k) for slot in range(slots) for k in list(range(1, dates)) + [0]]


def positions(dates, slots):
    places, sizes = {}, {}
    for slot, k in messages(dates, slots):
        which = max(k - (dates - 3), 0)
        places[slot, k] = (which, sizes.get(which, 0))
        sizes[which] = sizes.get(which, 0) + (2 if k else 1)
    return places


def routes(dates, slabs, slot, k):
    place = lambda d, t, core: (d * slabs + t) * 2 + core
    pairs = []
    for d in range(dates):
        for t in range(slabs):
            near = t ^ 1 if slot == 0 else ((t + 1) ^ 1) - 1
            for core in range(2):
                own = k > 0 and core == 0
                if own and slot == 0:
                    pairs.append((place(d, t, core), place(along(d, k, dates), t, core)))
                if not own and 0 <= near < slabs:
                    pairs.append((place(d, t, core), place(along(d, k, dates), near, core)))
    return pairs


def local(slabs, tokens, cloud_mask, day_of_year, query, key_weight, value_weight, conv_first, conv_second):
    tiles, rows, cols, dates, width = tokens.shape
    pixels = rows * cols
    slots = 1 if slabs <= 2 else 2
    swap = [(0, 1), (1, 0)]
    first = conv_first.reshape(3, 3 * width, -1)
    second = conv_second.reshape(3, 3 * width, -1)
    other = lax.ppermute(first, "head", swap)
    mine = attend(tokens, cloud_mask, day_of_year, query, key_weight, value_weight)
    theirs = lax.ppermute(mine, "head", swap)
    pieces = {}
    for (slot, k), (which, _) in positions(tiles, slots).items():
        block = jnp.stack([mine[k], theirs[k]]) if k > 0 else mine[:1]
        piece = lax.ppermute(block, ("date", "tile", "head"), routes(tiles, slabs, slot, k))
        pieces.setdefault(which, []).append(piece)
    got = [jnp.concatenate(pieces[which]) for which in sorted(pieces)]
    swapped = [lax.ppermute(part, "head", swap) for part in got]
    out = convolve(mine, theirs, got, swapped, first, other, second, pixels, cols, slabs, slots)
    return out.reshape(1, rows, cols, -1)


def solution(mesh):
    in_specs = (
        P("groups", "tile", None, "date", None),
        P("groups", "tile", None, "date"),
        P(("groups", "date")),
        P("head"),
        P(None, "head"),
        P(None, "head"),
        P(None, None, None, "head"),
        P(None, None, None, "head"),
    )
    out_specs = P(("groups", "date"), "tile", None, "head")
    body = functools.partial(local, mesh.shape["tile"])
    return jax.shard_map(body, mesh=mesh, in_specs=in_specs, out_specs=out_specs, check_vma=False)
```

```python
import functools
import math

import jax
import jax.numpy as jnp
from jax import lax
from jax.experimental import pallas as pl
from jax.experimental.pallas import tpu as pltpu
from jax.sharding import PartitionSpec as P

HSIZE = 32
LANES = 128
PENALTY = 6.0
LOG2E = math.log2(math.e)
F32 = jnp.float32
BF16 = jnp.bfloat16


def along(d, k, dates):
    if dates & (dates - 1):
        return (d + k) % dates
    rank, shift = d, 1
    while shift < dates:
        rank, shift = rank ^ (rank >> shift), 2 * shift
    rank = (rank + k) & (dates - 1)
    return rank ^ (rank >> 1)


def iota(shape, dim):
    return lax.broadcasted_iota(jnp.int32, shape, dim)


def split3(value):
    high = value.astype(BF16)
    rest = value - high.astype(F32)
    mid = rest.astype(BF16)
    low = (rest - mid.astype(F32)).astype(BF16)
    return high, mid, low


def same_head(rows):
    row = lax.rem(iota((rows, LANES), 0), LANES)
    return (row // HSIZE == iota((rows, LANES), 1) // HSIZE).astype(BF16)


def dot(a, b):
    return jnp.dot(a, b, preferred_element_type=F32)


def encoding_rows(days, dates, width):
    row, chan = iota((dates, width), 0), iota((dates, width), 1)
    even = lax.rem(chan, 2) == 0
    expo = (chan - lax.rem(chan, 2)).astype(F32) * F32(math.log(1000.0) / width)
    day = jnp.zeros((dates, width), F32)
    for t in range(dates):
        day = jnp.where(row == t, days[t].astype(F32), day)
    angle = day * jnp.exp(-expo)
    return jnp.where(even, jnp.sin(angle), jnp.cos(angle))


def fold_dates(value, join):
    pixels, dates, lanes = value.shape
    value = functools.reduce(join, [value[:, t : t + 8] for t in range(0, dates, 8)])
    for step in (1, 2, 4):
        value = value.reshape(-1, 2, 8, lanes)
        first, second = value[:, 0], value[:, 1]
        low = (iota(first.shape, 1) & step) == 0
        value = join(
            jnp.where(low, first, second),
            pltpu.roll(jnp.where(low, second, first), 8 - step, 1),
        )
    return value.reshape(pixels, lanes)


def pool(feats, table, weights, clear):
    pixels, dates = clear.shape
    width = feats.shape[-1]
    feats = feats.reshape(pixels, dates, width).astype(F32) + table[None]
    both = dot(feats.astype(BF16).reshape(pixels * dates, width), weights)
    score = both[:, 0:LANES] + (both[:, LANES : 2 * LANES] + both[:, 2 * LANES : 3 * LANES])
    vals = both[:, 3 * LANES : 4 * LANES].reshape(pixels, dates, LANES)
    cloud = F32(PENALTY * LOG2E) * (1.0 - clear.astype(F32))
    score = score.reshape(pixels, dates, LANES) - lax.broadcast_in_dim(
        cloud, (pixels, dates, LANES), (0, 1)
    )
    top = jnp.max(score, axis=1)
    expo = jnp.exp2(score - top[:, None, :])
    total = fold_dates(expo, jnp.add)
    summed = fold_dates(expo * vals, jnp.add)
    level = top + jnp.log(total) * F32(LOG2E)
    own = lax.rem(iota((pixels, LANES), 1), HSIZE) == iota((pixels, LANES), 0)
    packed = jnp.sum(jnp.where(own, level, 0.0), axis=0, keepdims=True)
    row = iota((16, LANES), 0)
    tail = jnp.zeros((16, LANES), F32)
    for place, piece in enumerate(split3(packed)):
        tail = jnp.where(row == place, piece.astype(F32), tail)
    return (summed / total).astype(BF16), tail.astype(BF16)


def pool_all(count, out, tokens, table, weights, clear):
    def one(i):
        part, tail = pool(tokens[i], table[...], weights[...], clear(i))
        pixels = part.shape[0]
        out[i, 0:pixels, :] = part
        out[i, pixels : pixels + 16, :] = tail

    if count <= 4:
        for i in range(count):
            one(i)
    else:
        pl.loop(0, count)(one)


def attend_kernel(
    dates, tokens_hbm, mask_hbm, days_hbm, query_hbm, keyw_hbm, valw_hbm, out,
    tokens, mask, weights, table, days, query, keyw, sems, token_sems,
):
    tiles, width = tokens.shape[0], tokens.shape[-1]
    date = lax.axis_index("date")
    columns = pl.ds(3 * LANES, LANES)
    small = [
        pltpu.make_async_copy(days_hbm, days, sems.at[0]),
        pltpu.make_async_copy(query_hbm, query, sems.at[1]),
        pltpu.make_async_copy(keyw_hbm, keyw, sems.at[2]),
        pltpu.make_async_copy(valw_hbm, weights.at[:, columns], sems.at[3]),
        pltpu.make_async_copy(mask_hbm, mask, sems.at[4]),
    ]
    for copy in (small[0], small[2], small[1]):
        copy.start()
    loads = [
        pltpu.make_async_copy(tokens_hbm.at[along(date, i, tiles)], tokens.at[i], token_sems.at[i]) for i in range(tiles)
    ]
    for copy in loads + small[3:]:
        copy.start()
    small[0].wait()
    table[...] = encoding_rows(days, dates, width)
    small[1].wait()
    small[2].wait()
    scaled = keyw[...].astype(F32) * (query[...] * F32(HSIZE**-0.5 * LOG2E))
    spread = same_head(LANES)
    high, mid, low = split3(scaled)
    folded = dot(high, spread) + (dot(mid, spread) + dot(low, spread))
    for place, piece in enumerate(split3(folded)):
        weights[:, place * LANES : (place + 1) * LANES] = piece
    small[3].wait()
    small[4].wait()
    for copy in loads:
        copy.wait()
    pool_all(tiles, out, tokens, table, weights, lambda i: mask[along(date, i, tiles)])


def attend(tokens, cloud_mask, day_of_year, query, key_weight, value_weight):
    tiles, rows, cols, dates, width = tokens.shape
    pixels = rows * cols
    tokens = tokens.reshape(tiles, pixels * dates, width)
    mask = cloud_mask.reshape(tiles, pixels, dates)
    return pl.pallas_call(
        functools.partial(attend_kernel, dates),
        in_specs=[pl.BlockSpec(memory_space=pltpu.HBM)] * 6,
        out_specs=pl.BlockSpec(memory_space=pltpu.VMEM),
        out_shape=pltpu.VMEM((tiles, pixels + 16, LANES), BF16),
        scratch_shapes=[
            pltpu.VMEM(tokens.shape, BF16),
            pltpu.VMEM(mask.shape, jnp.int32),
            pltpu.VMEM((width, 4 * LANES), BF16),
            pltpu.VMEM((dates, width), F32),
            pltpu.SMEM(day_of_year.shape, jnp.int32),
            pltpu.VMEM((1, LANES), F32),
            pltpu.VMEM((width, LANES), BF16),
            pltpu.SemaphoreType.DMA((5,)),
            pltpu.SemaphoreType.DMA((tiles,)),
        ],
        compiler_params=pltpu.CompilerParams(vmem_limit_bytes=60 * 2**20),
    )(tokens, mask, day_of_year, query.reshape(1, LANES), key_weight, value_weight)


def merge(blocks, pixels, start, count):
    own = lax.rem(iota((count, LANES), 1), HSIZE) == iota((count, LANES), 0) + start
    masked = []
    for _, tail in blocks:
        tail = tail.astype(F32)
        pieces = [jnp.where(own, tail[i : i + 1], 0.0).astype(BF16) for i in range(3)]
        masked.append(jnp.concatenate(pieces, axis=1))
    wide = dot(jnp.concatenate(masked, axis=0), same_head(3 * LANES))
    levels = [wide[i * count : (i + 1) * count] for i in range(len(blocks))]
    best = functools.reduce(jnp.maximum, levels)
    shares = [jnp.exp2(level - best) for level in levels]
    parts = [share * part.astype(F32) for share, (part, _) in zip(shares, blocks)]
    pooled = functools.reduce(jnp.add, parts) / functools.reduce(jnp.add, shares)
    return pooled.astype(BF16).astype(F32)


def columns(field, cols):
    count = field.shape[0]
    col = lax.rem(iota(field.shape, 0), cols)
    left = jnp.where(col == 0, 0.0, pltpu.roll(field, 1, 0))
    right = jnp.where(col == cols - 1, 0.0, pltpu.roll(field, count - 1, 0))
    return jnp.concatenate([left, field, right], axis=1).astype(BF16)


def stencil(field, kernel, cols):
    count = field.shape[0] - 2 * cols
    return sum(dot(field, kernel[a])[a * cols : a * cols + count] for a in range(3))


def convolve_kernel(pixels, cols, slabs, slots, mine, theirs, *refs):
    dates = mine.shape[0]
    slab, head = lax.axis_index("tile"), lax.axis_index("head")
    odd = lax.rem(slab, 2) == 1
    halo = 2 * cols

    def in_order(own, partner):
        return jnp.concatenate(
            [jnp.where(head == 0, own, partner), jnp.where(head == 0, partner, own)], axis=1
        )

    places = positions(dates, slots)
    parts = (len(refs) - 4) // 2
    got, swapped, (first, other, second, out) = refs[:parts], refs[parts:-4], refs[-4:]

    def block(core, slot, k, half, start, count):
        which, place = places[slot, k]
        if k > 0:
            place += 1 - half if core else half
        else:
            core = half
        return tuple(
            jnp.where(head == core, got[which][place, rows], swapped[which][place, rows])
            for rows in (pl.ds(start, count), pl.ds(pixels, 16))
        )

    def kept(half):
        return tuple(
            jnp.where(head == half, mine[0, rows], theirs[0, rows])
            for rows in (pl.ds(0, pixels), pl.ds(pixels, 16))
        )

    centre = jnp.concatenate(
        [
            merge([kept(half)] + [block(0, 0, k, half, 0, pixels) for k in range(1, dates)], pixels, 0, pixels)
            for half in range(2)
        ],
        axis=1,
    )

    def neighbour(slot):
        up = odd if slot == 0 else jnp.logical_not(odd)
        start = pl.multiple_of(jnp.where(up, pixels - halo, 0), 16)
        return jnp.concatenate(
            [
                merge([block(1, slot, k, half, start, halo) for k in range(dates)], pixels, start, halo)
                for half in range(2)
            ],
            axis=1,
        )

    one = neighbour(0)
    two = neighbour(1) if slots > 1 else one
    above = jnp.where(slab > 0, jnp.where(odd, one, two), 0.0)
    below = jnp.where(slab < slabs - 1, jnp.where(odd, two, one), 0.0)
    field = jnp.concatenate([above, centre, below], axis=0)
    wide = columns(field, cols)
    hidden = in_order(stencil(wide, first, cols), stencil(wide, other, cols))
    count = pixels + 2 * cols
    row = iota(hidden.shape, 0)
    inside = jnp.logical_and(
        jnp.logical_or(row >= cols, slab > 0), jnp.logical_or(row < count - cols, slab < slabs - 1)
    )
    hidden = jnp.where(inside, jnp.maximum(hidden, 0.0), 0.0).astype(BF16).astype(F32)
    out[...] = stencil(columns(hidden, cols), second, cols).astype(BF16)


def convolve(mine, theirs, got, swapped, first, other, second, pixels, cols, slabs, slots):
    return pl.pallas_call(
        functools.partial(convolve_kernel, pixels, cols, slabs, slots),
        in_specs=[pl.BlockSpec(memory_space=pltpu.VMEM)] * (5 + 2 * len(got)),
        out_specs=pl.BlockSpec(memory_space=pltpu.VMEM),
        out_shape=jax.ShapeDtypeStruct((pixels, second.shape[-1]), BF16),
        compiler_params=pltpu.CompilerParams(vmem_limit_bytes=32 * 2**20),
    )(mine, theirs, *got, *swapped, first, other, second)


def messages(dates, slots):
    return [(slot, k) for slot in range(slots) for k in list(range(1, dates)) + [0]]


def positions(dates, slots):
    places, sizes = {}, {}
    for slot, k in messages(dates, slots):
        which = max(k - (dates - 3), 0)
        places[slot, k] = (which, sizes.get(which, 0))
        sizes[which] = sizes.get(which, 0) + (2 if k else 1)
    return places


def routes(dates, slabs, slot, k):
    place = lambda d, t, core: (d * slabs + t) * 2 + core
    pairs = []
    for d in range(dates):
        for t in range(slabs):
            near = t ^ 1 if slot == 0 else ((t + 1) ^ 1) - 1
            for core in range(2):
                own = k > 0 and core == 0
                if own and slot == 0:
                    pairs.append((place(d, t, core), place(along(d, k, dates), t, core)))
                if not own and 0 <= near < slabs:
                    pairs.append((place(d, t, core), place(along(d, k, dates), near, core)))
    return pairs


def local(slabs, tokens, cloud_mask, day_of_year, query, key_weight, value_weight, conv_first, conv_second):
    tiles, rows, cols, dates, width = tokens.shape
    pixels = rows * cols
    slots = 1 if slabs <= 2 else 2
    swap = [(0, 1), (1, 0)]
    first = conv_first.reshape(3, 3 * width, -1)
    second = conv_second.reshape(3, 3 * width, -1)
    other = lax.ppermute(first, "head", swap)
    mine = attend(tokens, cloud_mask, day_of_year, query, key_weight, value_weight)
    theirs = lax.ppermute(mine, "head", swap)
    pieces = {}
    for (slot, k), (which, _) in positions(tiles, slots).items():
        block = jnp.stack([mine[k], theirs[k]]) if k > 0 else mine[:1]
        piece = lax.ppermute(block, ("date", "tile", "head"), routes(tiles, slabs, slot, k))
        pieces.setdefault(which, []).append(piece)
    got = [jnp.concatenate(pieces[which]) for which in sorted(pieces)]
    swapped = [lax.ppermute(part, "head", swap) for part in got]
    out = convolve(mine, theirs, got, swapped, first, other, second, pixels, cols, slabs, slots)
    return out.reshape(1, rows, cols, -1)


def solution(mesh):
    in_specs = (
        P("groups", "tile", None, "date", None),
        P("groups", "tile", None, "date"),
        P(("groups", "date")),
        P("head"),
        P(None, "head"),
        P(None, "head"),
        P(None, None, None, "head"),
        P(None, None, None, "head"),
    )
    out_specs = P(("groups", "date"), "tile", None, "head")
    body = functools.partial(local, mesh.shape["tile"])
    return jax.shard_map(body, mesh=mesh, in_specs=in_specs, out_specs=out_specs, check_vma=False)
```

```python
import functools
import math

import jax
import jax.numpy as jnp
from jax import lax
from jax.experimental import pallas as pl
from jax.experimental.pallas import tpu as pltpu
from jax.sharding import PartitionSpec as P

HSIZE = 32
LANES = 128
PENALTY = 6.0
LOG2E = math.log2(math.e)
F32 = jnp.float32
BF16 = jnp.bfloat16


def along(d, k, dates):
    if dates & (dates - 1):
        return (d + k) % dates
    rank, shift = d, 1
    while shift < dates:
        rank, shift = rank ^ (rank >> shift), 2 * shift
    rank = (rank + k) & (dates - 1)
    return rank ^ (rank >> 1)


def iota(shape, dim):
    return lax.broadcasted_iota(jnp.int32, shape, dim)


def split3(value):
    high = value.astype(BF16)
    rest = value - high.astype(F32)
    mid = rest.astype(BF16)
    low = (rest - mid.astype(F32)).astype(BF16)
    return high, mid, low


def same_head(rows):
    row = lax.rem(iota((rows, LANES), 0), LANES)
    return (row // HSIZE == iota((rows, LANES), 1) // HSIZE).astype(BF16)


def dot(a, b):
    return jnp.dot(a, b, preferred_element_type=F32)


def encoding_rows(days, dates, width):
    row, chan = iota((dates, width), 0), iota((dates, width), 1)
    even = lax.rem(chan, 2) == 0
    expo = (chan - lax.rem(chan, 2)).astype(F32) * F32(math.log(1000.0) / width)
    day = jnp.zeros((dates, width), F32)
    for t in range(dates):
        day = jnp.where(row == t, days[t].astype(F32), day)
    angle = day * jnp.exp(-expo)
    return jnp.where(even, jnp.sin(angle), jnp.cos(angle))


def fold_dates(value, join):
    pixels, dates, lanes = value.shape
    value = functools.reduce(join, [value[:, t : t + 8] for t in range(0, dates, 8)])
    for step in (1, 2, 4):
        value = value.reshape(-1, 2, 8, lanes)
        first, second = value[:, 0], value[:, 1]
        low = (iota(first.shape, 1) & step) == 0
        value = join(
            jnp.where(low, first, second),
            pltpu.roll(jnp.where(low, second, first), 8 - step, 1),
        )
    return value.reshape(pixels, lanes)


def pool(feats, table, weights, clear):
    pixels, dates = clear.shape
    width = feats.shape[-1]
    feats = feats.reshape(pixels, dates, width).astype(F32) + table[None]
    both = dot(feats.astype(BF16).reshape(pixels * dates, width), weights)
    score = both[:, 0:LANES] + (both[:, LANES : 2 * LANES] + both[:, 2 * LANES : 3 * LANES])
    vals = both[:, 3 * LANES : 4 * LANES].reshape(pixels, dates, LANES)
    cloud = F32(PENALTY * LOG2E) * (1.0 - clear.astype(F32))
    score = score.reshape(pixels, dates, LANES) - lax.broadcast_in_dim(
        cloud, (pixels, dates, LANES), (0, 1)
    )
    top = jnp.max(score, axis=1)
    expo = jnp.exp2(score - top[:, None, :])
    total = fold_dates(expo, jnp.add)
    summed = fold_dates(expo * vals, jnp.add)
    level = top + jnp.log(total) * F32(LOG2E)
    own = lax.rem(iota((pixels, LANES), 1), HSIZE) == iota((pixels, LANES), 0)
    packed = jnp.sum(jnp.where(own, level, 0.0), axis=0, keepdims=True)
    row = iota((16, LANES), 0)
    tail = jnp.zeros((16, LANES), F32)
    for place, piece in enumerate(split3(packed)):
        tail = jnp.where(row == place, piece.astype(F32), tail)
    return (summed / total).astype(BF16), tail.astype(BF16)


def pool_all(count, out, tokens, table, weights, clear):
    def one(i):
        part, tail = pool(tokens[i], table[...], weights[...], clear(i))
        pixels = part.shape[0]
        out[i, 0:pixels, :] = part
        out[i, pixels : pixels + 16, :] = tail

    if count <= 4:
        for i in range(count):
            one(i)
    else:
        pl.loop(0, count)(one)


def attend_kernel(
    dates, tokens_hbm, mask_hbm, days_hbm, query_hbm, keyw_hbm, valw_hbm, out,
    tokens, mask, weights, table, days, query, keyw, sems, token_sems,
):
    tiles, width = tokens.shape[0], tokens.shape[-1]
    date = lax.axis_index("date")
    columns = pl.ds(3 * LANES, LANES)
    small = [
        pltpu.make_async_copy(days_hbm, days, sems.at[0]),
        pltpu.make_async_copy(query_hbm, query, sems.at[1]),
        pltpu.make_async_copy(keyw_hbm, keyw, sems.at[2]),
        pltpu.make_async_copy(valw_hbm, weights.at[:, columns], sems.at[3]),
        pltpu.make_async_copy(mask_hbm, mask, sems.at[4]),
    ]
    for copy in (small[0], small[2], small[1]):
        copy.start()
    loads = [
        pltpu.make_async_copy(tokens_hbm.at[along(date, i, tiles)], tokens.at[i], token_sems.at[i]) for i in range(tiles)
    ]
    for i, copy in enumerate(loads + small[3:]):
        copy.start(priority=i % 2)
    small[0].wait()
    table[...] = encoding_rows(days, dates, width)
    small[1].wait()
    small[2].wait()
    scaled = keyw[...].astype(F32) * (query[...] * F32(HSIZE**-0.5 * LOG2E))
    spread = same_head(LANES)
    high, mid, low = split3(scaled)
    folded = dot(high, spread) + (dot(mid, spread) + dot(low, spread))
    for place, piece in enumerate(split3(folded)):
        weights[:, place * LANES : (place + 1) * LANES] = piece
    small[3].wait()
    small[4].wait()
    for copy in loads:
        copy.wait()
    pool_all(tiles, out, tokens, table, weights, lambda i: mask[along(date, i, tiles)])


def attend(tokens, cloud_mask, day_of_year, query, key_weight, value_weight):
    tiles, rows, cols, dates, width = tokens.shape
    pixels = rows * cols
    tokens = tokens.reshape(tiles, pixels * dates, width)
    mask = cloud_mask.reshape(tiles, pixels, dates)
    return pl.pallas_call(
        functools.partial(attend_kernel, dates),
        in_specs=[pl.BlockSpec(memory_space=pltpu.HBM)] * 6,
        out_specs=pl.BlockSpec(memory_space=pltpu.VMEM),
        out_shape=pltpu.VMEM((tiles, pixels + 16, LANES), BF16),
        scratch_shapes=[
            pltpu.VMEM(tokens.shape, BF16),
            pltpu.VMEM(mask.shape, jnp.int32),
            pltpu.VMEM((width, 4 * LANES), BF16),
            pltpu.VMEM((dates, width), F32),
            pltpu.SMEM(day_of_year.shape, jnp.int32),
            pltpu.VMEM((1, LANES), F32),
            pltpu.VMEM((width, LANES), BF16),
            pltpu.SemaphoreType.DMA((5,)),
            pltpu.SemaphoreType.DMA((tiles,)),
        ],
        compiler_params=pltpu.CompilerParams(vmem_limit_bytes=60 * 2**20),
    )(tokens, mask, day_of_year, query.reshape(1, LANES), key_weight, value_weight)


def merge(blocks, pixels, start, count):
    own = lax.rem(iota((count, LANES), 1), HSIZE) == iota((count, LANES), 0) + start
    masked = []
    for _, tail in blocks:
        tail = tail.astype(F32)
        pieces = [jnp.where(own, tail[i : i + 1], 0.0).astype(BF16) for i in range(3)]
        masked.append(jnp.concatenate(pieces, axis=1))
    wide = dot(jnp.concatenate(masked, axis=0), same_head(3 * LANES))
    levels = [wide[i * count : (i + 1) * count] for i in range(len(blocks))]
    best = functools.reduce(jnp.maximum, levels)
    shares = [jnp.exp2(level - best) for level in levels]
    parts = [share * part.astype(F32) for share, (part, _) in zip(shares, blocks)]
    pooled = functools.reduce(jnp.add, parts) / functools.reduce(jnp.add, shares)
    return pooled.astype(BF16).astype(F32)


def columns(field, cols):
    count = field.shape[0]
    col = lax.rem(iota(field.shape, 0), cols)
    left = jnp.where(col == 0, 0.0, pltpu.roll(field, 1, 0))
    right = jnp.where(col == cols - 1, 0.0, pltpu.roll(field, count - 1, 0))
    return jnp.concatenate([left, field, right], axis=1).astype(BF16)


def stencil(field, kernel, cols):
    count = field.shape[0] - 2 * cols
    return sum(dot(field, kernel[a])[a * cols : a * cols + count] for a in range(3))


def convolve_kernel(pixels, cols, slabs, slots, mine, theirs, *refs):
    dates = mine.shape[0]
    slab, head = lax.axis_index("tile"), lax.axis_index("head")
    odd = lax.rem(slab, 2) == 1
    halo = 2 * cols

    def in_order(own, partner):
        return jnp.concatenate(
            [jnp.where(head == 0, own, partner), jnp.where(head == 0, partner, own)], axis=1
        )

    places = positions(dates, slots)
    parts = (len(refs) - 4) // 2
    got, swapped, (first, other, second, out) = refs[:parts], refs[parts:-4], refs[-4:]

    def block(core, slot, k, half, start, count):
        which, place = places[slot, k]
        if k > 0:
            place += 1 - half if core else half
        else:
            core = half
        return tuple(
            jnp.where(head == core, got[which][place, rows], swapped[which][place, rows])
            for rows in (pl.ds(start, count), pl.ds(pixels, 16))
        )

    def kept(half):
        return tuple(
            jnp.where(head == half, mine[0, rows], theirs[0, rows])
            for rows in (pl.ds(0, pixels), pl.ds(pixels, 16))
        )

    centre = jnp.concatenate(
        [
            merge([kept(half)] + [block(0, 0, k, half, 0, pixels) for k in range(1, dates)], pixels, 0, pixels)
            for half in range(2)
        ],
        axis=1,
    )

    def neighbour(slot):
        up = odd if slot == 0 else jnp.logical_not(odd)
        start = pl.multiple_of(jnp.where(up, pixels - halo, 0), 16)
        return jnp.concatenate(
            [
                merge([block(1, slot, k, half, start, halo) for k in range(dates)], pixels, start, halo)
                for half in range(2)
            ],
            axis=1,
        )

    one = neighbour(0)
    two = neighbour(1) if slots > 1 else one
    above = jnp.where(slab > 0, jnp.where(odd, one, two), 0.0)
    below = jnp.where(slab < slabs - 1, jnp.where(odd, two, one), 0.0)
    field = jnp.concatenate([above, centre, below], axis=0)
    wide = columns(field, cols)
    hidden = in_order(stencil(wide, first, cols), stencil(wide, other, cols))
    count = pixels + 2 * cols
    row = iota(hidden.shape, 0)
    inside = jnp.logical_and(
        jnp.logical_or(row >= cols, slab > 0), jnp.logical_or(row < count - cols, slab < slabs - 1)
    )
    hidden = jnp.where(inside, jnp.maximum(hidden, 0.0), 0.0).astype(BF16).astype(F32)
    out[...] = stencil(columns(hidden, cols), second, cols).astype(BF16)


def convolve(mine, theirs, got, swapped, first, other, second, pixels, cols, slabs, slots):
    return pl.pallas_call(
        functools.partial(convolve_kernel, pixels, cols, slabs, slots),
        in_specs=[pl.BlockSpec(memory_space=pltpu.VMEM)] * (5 + 2 * len(got)),
        out_specs=pl.BlockSpec(memory_space=pltpu.VMEM),
        out_shape=jax.ShapeDtypeStruct((pixels, second.shape[-1]), BF16),
        compiler_params=pltpu.CompilerParams(vmem_limit_bytes=32 * 2**20),
    )(mine, theirs, *got, *swapped, first, other, second)


def messages(dates, slots):
    return [(slot, k) for slot in range(slots) for k in list(range(1, dates)) + [0]]


def positions(dates, slots):
    places, sizes = {}, {}
    for slot, k in messages(dates, slots):
        which = max(k - (dates - 3), 0)
        places[slot, k] = (which, sizes.get(which, 0))
        sizes[which] = sizes.get(which, 0) + (2 if k else 1)
    return places


def routes(dates, slabs, slot, k):
    place = lambda d, t, core: (d * slabs + t) * 2 + core
    pairs = []
    for d in range(dates):
        for t in range(slabs):
            near = t ^ 1 if slot == 0 else ((t + 1) ^ 1) - 1
            for core in range(2):
                own = k > 0 and core == 0
                if own and slot == 0:
                    pairs.append((place(d, t, core), place(along(d, k, dates), t, core)))
                if not own and 0 <= near < slabs:
                    pairs.append((place(d, t, core), place(along(d, k, dates), near, core)))
    return pairs


def local(slabs, tokens, cloud_mask, day_of_year, query, key_weight, value_weight, conv_first, conv_second):
    tiles, rows, cols, dates, width = tokens.shape
    pixels = rows * cols
    slots = 1 if slabs <= 2 else 2
    swap = [(0, 1), (1, 0)]
    first = conv_first.reshape(3, 3 * width, -1)
    second = conv_second.reshape(3, 3 * width, -1)
    other = lax.ppermute(first, "head", swap)
    mine = attend(tokens, cloud_mask, day_of_year, query, key_weight, value_weight)
    theirs = lax.ppermute(mine, "head", swap)
    pieces = {}
    for (slot, k), (which, _) in positions(tiles, slots).items():
        block = jnp.stack([mine[k], theirs[k]]) if k > 0 else mine[:1]
        piece = lax.ppermute(block, ("date", "tile", "head"), routes(tiles, slabs, slot, k))
        pieces.setdefault(which, []).append(piece)
    got = [jnp.concatenate(pieces[which]) for which in sorted(pieces)]
    swapped = [lax.ppermute(part, "head", swap) for part in got]
    out = convolve(mine, theirs, got, swapped, first, other, second, pixels, cols, slabs, slots)
    return out.reshape(1, rows, cols, -1)


def solution(mesh):
    in_specs = (
        P("groups", "tile", None, "date", None),
        P("groups", "tile", None, "date"),
        P(("groups", "date")),
        P("head"),
        P(None, "head"),
        P(None, "head"),
        P(None, None, None, "head"),
        P(None, None, None, "head"),
    )
    out_specs = P(("groups", "date"), "tile", None, "head")
    body = functools.partial(local, mesh.shape["tile"])
    return jax.shard_map(body, mesh=mesh, in_specs=in_specs, out_specs=out_specs, check_vma=False)
```
